32 devices in a mesh: dp: 16 (over z, x, core), mp: 2 (over y).
Axes of the slice: x: 2, y: 2, z: 4, core: 2. Of those that a mesh axis runs over, the one named last changes fastest.
Arguments:
- tokens: bfloat16 [8192, 2048], P(('dp', 'mp')), may hold values from -6 to 6
- norm_gain: bfloat16 [2048], P('dp'), may hold values from 0.5 to 1.5
- norm_shift: bfloat16 [2048], P('dp'), may hold values from -1.25 to 1.25
- in_weight: bfloat16 [3, 2048, 2048], P(None, 'dp', 'mp'), may hold values from -0.125 to 0.125
- in_bias: bfloat16 [3, 2048], P(None, ('mp', 'dp')), may hold values from -1.25 to 1.25
- out_weight: bfloat16 [2048, 2048], P('dp', 'mp'), may hold values from -0.375 to 0.375
- out_bias: bfloat16 [2048], P('dp'), may hold values from -1.25 to 1.25
- up_weight: bfloat16 [2048, 8192], P('dp', 'mp'), may hold values from -0.125 to 0.125
- up_bias: bfloat16 [8192], P(('mp', 'dp')), may hold values from -1.25 to 1.25
- down_weight: bfloat16 [2048, 8192], P('dp', 'mp'), may hold values from -0.0625 to 0.0625
- down_bias: bfloat16 [2048], P('dp'), may hold values from -1.25 to 1.25
- cotangent: bfloat16 [8192, 2048], P(('dp', 'mp')), may hold values from -6 to 6
Outputs:
- result: bfloat16 [8192, 2048], P(('dp', 'mp'))
- grad_tokens: float32 [8192, 2048], P(('dp', 'mp'))
- grad_gain: float32 [2048], P('dp')
- grad_shift: float32 [2048], P('dp')
- grad_in_weight: float32 [3, 2048, 2048], P(None, 'dp', 'mp')
- grad_in_bias: float32 [3, 2048], P(None, ('mp', 'dp'))
- grad_out_weight: float32 [2048, 2048], P('dp', 'mp')
- grad_out_bias: float32 [2048], P('dp')
- grad_up_weight: float32 [2048, 8192], P('dp', 'mp')
- grad_up_bias: float32 [8192], P(('mp', 'dp'))
- grad_down_weight: float32 [2048, 8192], P('dp', 'mp')
- grad_down_bias: float32 [2048], P('dp')
The draws below stay inside these ranges and needn't reach their ends.
All inputs are finite; a program needn't handle non-finite values.
Results may differ from the reference program's by a relative error of at most 0.0095.
Values may be sent and summed in bfloat16 or wider, within the bound.
A program may use at most 384 MiB of HBM per device.

```python
import math
import jax
import jax.numpy as jnp
from jax import lax

D = 2048
FF = 8192
HEADS = 32
HEAD = 64
ROT = 32
SEQ = 512
TOKENS = 8192
N_DP = 16


def with_spikes(entries, own_key, source, target, blocks, factor):
    owner, partner = [(jnp.arange(entries.shape[axis_at]) // (entries.shape[axis_at] // blocks)).reshape([-1 if axis == axis_at else 1 for axis in range(entries.ndim)]) for axis_at in (source, target)]
    chosen = jax.random.permutation(own_key, blocks)[partner]
    strong = (owner == chosen) | (owner == (partner + blocks // 2) % blocks)
    return jnp.where(strong, factor * entries, entries)


def block_levels(own_key, dims, cuts, smallest, high):
    level = 1.0
    for dim, blocks in cuts:
        heights = jax.random.uniform(jax.random.fold_in(jax.random.fold_in(own_key, 6), dim), (blocks,), jnp.float32, smallest / len(cuts), high / len(cuts))
        level = level * jnp.repeat(jnp.exp(heights), dims[dim] // blocks).reshape((-1,) + (1,) * (len(dims) - 1 - dim))
    return level


def gaussian(rng, dims, deviation, limit, split=(), kind=jnp.bfloat16):
    factor_of = block_levels(rng, dims, split, -0.22, 0.18) if split else 1.0
    entries = jax.random.normal(rng, dims, jnp.float32) * deviation * factor_of
    return jnp.minimum(jnp.maximum(entries, -limit), limit).astype(kind)


def heavy_noise(key, dims, deviation, most, split, heavy, kind=jnp.bfloat16):
    drawn = deviation * jax.random.normal(key, dims, jnp.float32)
    if split:
        drawn = drawn * block_levels(key, dims, split, -0.22, 0.18)
    return jnp.clip(with_spikes(drawn, jax.random.fold_in(key, 3), *heavy), -most, most).astype(kind)


def setup_inputs(seed: int = 0) -> dict:
    arg_keys = jax.random.split(jax.random.key(seed), 13)
    return {
        "tokens": heavy_noise(arg_keys[0], (TOKENS, D), 1.0, 6.0, ((0, 32),), (0, 1, 32, 2.75)),
        "norm_gain": jnp.clip(1.0 + 0.1 * jax.random.normal(arg_keys[1], (D,), jnp.float32), 0.5, 1.5).astype(jnp.bfloat16),
        "norm_shift": gaussian(arg_keys[2], (D,), 0.2, 1.25, ((0, 16),)),
        "in_weight": gaussian(arg_keys[3], (3, D, D), D ** -0.5, 0.125, ((1, 16), (2, 2))),
        "in_bias": gaussian(arg_keys[4], (3, D), 0.2, 1.25, ((1, 32),)),
        "out_weight": gaussian(arg_keys[5], (D, D), (D // 8) ** -0.5, 0.375, ((0, 16), (1, 2))),
        "out_bias": gaussian(arg_keys[6], (D,), 0.2, 1.25, ((0, 16),)),
        "up_weight": gaussian(arg_keys[7], (D, FF), D ** -0.5, 0.125, ((0, 16), (1, 2))),
        "up_bias": gaussian(arg_keys[8], (FF,), 0.2, 1.25, ((0, 32),)),
        "down_weight": gaussian(arg_keys[9], (D, FF), FF ** -0.5, 0.0625, ((0, 16), (1, 2))),
        "down_bias": gaussian(arg_keys[10], (D,), 0.2, 1.25, ((0, 16),)),
        "cotangent": heavy_noise(arg_keys[11], (TOKENS, D), 1.0, 6.0, ((0, 32),), (0, 1, 32, 2.75)),
    }


@jax.custom_vjp
def low(v):
    return lax.optimization_barrier(v.astype(jnp.bfloat16)).astype(jnp.float32)

@jax.custom_vjp
def low_back(v):
    return v

def low_keep(v):
    return (low(v), None)

def low_pass(kept, grad):
    return (grad,)

def back_keep(v):
    return (v, None)

def back_low(kept, grad):
    return (low(grad),)
low.defvjp(low_keep, low_pass)
low_back.defvjp(back_keep, back_low)
highest = lax.Precision.HIGHEST
norm_eps = 1e-05

def both_ways(values):
    return low_back(low(values))

def normalize(rows):
    middle = lax.optimization_barrier(jnp.mean(rows, axis=-1, keepdims=True))
    centered = rows - middle
    spread = lax.optimization_barrier(jnp.mean(centered * centered, axis=-1, keepdims=True))
    inv_spread = lax.rsqrt(spread + norm_eps)
    return (centered * inv_spread, inv_spread)

def rotary_tables(length):
    half_rot = ROT // 2
    position = jnp.arange(length, dtype=jnp.float32)
    freqs = jnp.exp(jnp.arange(half_rot, dtype=jnp.float32) * (-math.log(10000.0) / half_rot))
    angles = position[:, None] * freqs[None, :]
    angles = jnp.concatenate([angles, angles], axis=1)
    return (jnp.cos(angles), jnp.sin(angles))

def rotate(vectors, cosine, sine):
    half_rot = ROT // 2
    turned = vectors[..., :ROT]
    swapped = jnp.concatenate([-turned[..., half_rot:], turned[..., :half_rot]], axis=-1)
    turned = turned * cosine[:, None, :] + swapped * sine[:, None, :]
    return jnp.concatenate([turned, vectors[..., ROT:]], axis=-1)

def layer(batch, params):
    norm_gain, norm_shift, in_weight, in_bias, out_weight, out_bias, up_weight, up_bias, down_weight, down_bias = params
    groups = batch.shape[0]
    length = batch.shape[1]
    unit_rows = normalize(batch)[0]
    normed = low(unit_rows * norm_gain + norm_shift)
    projected = jnp.einsum('gsd,kde->kgse', normed, in_weight, precision=highest) + in_bias[:, None, None, :]
    projected = low_back(projected).reshape(3, groups, length, HEADS, HEAD)
    cosine, sine = rotary_tables(length)
    queries = both_ways(rotate(projected[0], cosine, sine))
    keys = both_ways(rotate(projected[1], cosine, sine))
    values = low(projected[2])
    scores = jnp.einsum('gqhe,gkhe->ghqk', queries, keys, precision=highest) * (1.0 / math.sqrt(HEAD))
    scores = low_back(scores)
    row_ids = lax.broadcasted_iota(jnp.int32, (length, length), 0)
    col_ids = lax.broadcasted_iota(jnp.int32, (length, length), 1)
    scores = jnp.where(col_ids <= row_ids, scores, -1e+30)
    top_score = lax.optimization_barrier(jnp.max(scores, axis=-1, keepdims=True))
    powers = jnp.exp(scores - top_score)
    weights = low(powers / lax.optimization_barrier(jnp.sum(powers, axis=-1, keepdims=True)))
    mixed = jnp.einsum('ghqk,gkhe->gqhe', weights, values, precision=highest)
    mixed = both_ways(mixed.reshape(groups, length, HEADS * HEAD))
    attended = jnp.einsum('gse,de->gsd', mixed, out_weight, precision=highest)
    preact = low_back(jnp.einsum('gsd,df->gsf', normed, up_weight, precision=highest) + up_bias)
    activated = low(jax.nn.gelu(preact, approximate=True))
    feedfwd = jnp.einsum('gsf,df->gsd', activated, down_weight, precision=highest)
    return batch + attended + feedfwd + out_bias + down_bias

def reference(tokens, norm_gain, norm_shift, in_weight, in_bias, out_weight, out_bias, up_weight, up_bias, down_weight, down_bias, cotangent):
    params = tuple((entry.astype(jnp.float32) for entry in (norm_gain, norm_shift, in_weight, in_bias, out_weight, out_bias, up_weight, up_bias, down_weight, down_bias)))
    group_count = math.gcd(N_DP, max(1, 4096 // SEQ))
    batches = tokens.astype(jnp.float32).reshape(N_DP // group_count, group_count, SEQ, D)

    def forward(batches, params):

        def one_group(batch):
            return layer(batch, params)
        return lax.map(jax.checkpoint(one_group), batches)
    outcome, pull = jax.vjp(forward, batches, params)
    grad_batches, grads = pull(cotangent.astype(jnp.float32).reshape(outcome.shape))
    return (outcome.reshape(TOKENS, D).astype(jnp.bfloat16), grad_batches.reshape(TOKENS, D), grads[0], grads[1], grads[2], grads[3], grads[4], grads[5], grads[6], grads[7], grads[8], grads[9])
```

```python
import math

import jax
import jax.numpy as jnp
from jax import lax
from jax.sharding import PartitionSpec as P

HEAD = 64
ROT = 32
QUARTERS = 4
norm_eps = 1e-05
F32 = jnp.float32
BF16 = jnp.bfloat16


def normalize(rows):
    middle = jnp.mean(rows, axis=-1, keepdims=True)
    centered = rows - middle
    spread = jnp.mean(centered * centered, axis=-1, keepdims=True)
    inv_spread = lax.rsqrt(spread + norm_eps)
    return (centered * inv_spread, inv_spread)


def rotary_tables(length):
    half_rot = ROT // 2
    position = jnp.arange(length, dtype=F32)
    freqs = jnp.exp(jnp.arange(half_rot, dtype=F32) * (-math.log(10000.0) / half_rot))
    angles = position[:, None] * freqs[None, :]
    angles = jnp.concatenate([angles, angles], axis=1)
    return (jnp.cos(angles), jnp.sin(angles))


def rotate(vectors, cosine, sine):
    half_rot = ROT // 2
    turned = vectors[..., :ROT]
    swapped = jnp.concatenate([-turned[..., half_rot:], turned[..., :half_rot]], axis=-1)
    turned = turned * cosine[:, None, :] + swapped * sine[:, None, :]
    return jnp.concatenate([turned, vectors[..., ROT:]], axis=-1)


def attend(queries, keys):
    length = queries.shape[1]
    scores = jnp.einsum("gqhe,gkhe->ghqk", queries, keys, preferred_element_type=F32) * (
        1.0 / math.sqrt(HEAD)
    )
    row_ids = lax.broadcasted_iota(jnp.int32, (length, length), 0)
    col_ids = lax.broadcasted_iota(jnp.int32, (length, length), 1)
    scores = jnp.where((col_ids <= row_ids)[None, None], scores, -1e30)
    top_score = jnp.max(scores, axis=-1, keepdims=True)
    powers = jnp.exp(scores - top_score)
    return powers / jnp.sum(powers, axis=-1, keepdims=True)


def smooth_gate(inputs):
    return jax.nn.gelu(inputs, approximate=True)


def per_device(
    tokens,
    norm_gain,
    norm_shift,
    in_weight,
    in_bias,
    out_weight,
    out_bias,
    up_weight,
    up_bias,
    down_weight,
    down_bias,
    cotangent,
):
    n_dp = lax.axis_size("dp")
    n_mp = lax.axis_size("mp")
    lines = n_dp // QUARTERS
    dp = lax.axis_index("dp")
    mp = lax.axis_index("mp")
    quarter = dp % QUARTERS
    line = dp // QUARTERS
    line_groups = [[k * QUARTERS + q for k in range(lines)] for q in range(QUARTERS)]
    team = QUARTERS * n_mp
    team_groups = [[k * team + i for i in range(team)] for k in range(lines)]
    own_rows, width = tokens.shape

    def pick(array, index, axis):
        return lax.dynamic_index_in_dim(array, index, axis, keepdims=False)

    def place(buffer, piece, index, axis):
        return lax.dynamic_update_index_in_dim(buffer, piece, index, axis)

    def swap_quarters(array, axis):
        got = []
        for j in range(QUARTERS):
            piece = pick(array, quarter ^ j, axis)
            if j:
                piece = lax.ppermute(piece, "dp", [(d, d ^ j) for d in range(n_dp)])
            got.append(piece)
        return got

    def gather_lines(piece):
        ups, downs = [piece], [piece]
        for k in range(1, lines):
            up_pairs = [
                (d, d + QUARTERS)
                for d in range(n_dp)
                if k - 1 <= d // QUARTERS < lines - 1
            ]
            down_pairs = [(n_dp - 1 - a, n_dp - 1 - b) for a, b in up_pairs]
            ups.append(lax.ppermute(ups[-1], "dp", up_pairs))
            downs.append(lax.ppermute(downs[-1], "dp", down_pairs))
        whole = jnp.zeros((lines,) + piece.shape, piece.dtype)
        whole = place(whole, piece, line, 0)
        for k in range(1, lines):
            whole = place(
                whole,
                jnp.where(line >= k, ups[k], downs[lines - k]),
                (line - k) % lines,
                0,
            )
        return whole.reshape((-1,) + piece.shape[1:])

    def gather_weight(block):
        got = swap_quarters(block, 1)
        rows = jnp.zeros((QUARTERS,) + got[0].shape, block.dtype)
        for j in range(QUARTERS):
            rows = place(rows, got[j], quarter ^ j, 0)
        return gather_lines(rows.reshape((-1,) + got[0].shape[1:]))

    def scatter_grad(grad):
        mine = lax.psum_scatter(
            grad.astype(BF16),
            "dp",
            scatter_dimension=0,
            tiled=True,
            axis_index_groups=line_groups,
        )
        got = swap_quarters(mine.reshape((QUARTERS, -1) + mine.shape[1:]), 0)
        cols = jnp.zeros((got[0].shape[0], QUARTERS) + got[0].shape[1:], F32)
        for j in range(QUARTERS):
            cols = place(cols, got[j].astype(F32), quarter ^ j, 1)
        return cols

    def gather_team(rows):
        return lax.all_gather(
            rows, ("dp", "mp"), axis=0, tiled=True, axis_index_groups=team_groups
        )

    def scatter_team(partial):
        parts = partial.astype(BF16).reshape(QUARTERS // 2, 2, n_mp, own_rows, width)
        core = dp % 2
        half = (dp // 2) % (QUARTERS // 2)
        mine = pick(parts, core, 1)
        got = lax.ppermute(pick(parts, 1 - core, 1), "dp", [(d, d ^ 1) for d in range(n_dp)])
        pair = (mine.astype(F32) + got.astype(F32)).astype(BF16)
        total = pick(pick(pair, half, 0), mp, 0).astype(F32)
        for a in range(QUARTERS // 2):
            for b in range(n_mp):
                if a or b:
                    piece = pick(pick(pair, half ^ a, 0), (mp + b) % n_mp, 0)
                    pairs = [
                        (d * n_mp + m, (d ^ (2 * a)) * n_mp + (m + b) % n_mp)
                        for d in range(n_dp)
                        for m in range(n_mp)
                    ]
                    total = total + lax.ppermute(piece, ("dp", "mp"), pairs).astype(F32)
        return total

    small = jnp.concatenate(
        [norm_gain, norm_shift, out_bias, down_bias, in_bias.reshape(-1), up_bias]
    )
    small = lax.all_gather(small, "dp", axis=0, tiled=False).astype(F32)
    each = norm_gain.shape[0]
    full_gain = small[:, :each].reshape(-1)
    full_shift = small[:, each : 2 * each].reshape(-1)
    full_out_bias = small[:, 2 * each : 3 * each].reshape(-1)
    full_down_bias = small[:, 3 * each : 4 * each].reshape(-1)
    in_each = in_bias.shape[1]
    up_each = up_bias.shape[0]
    in_part = small[:, 4 * each : 4 * each + 3 * in_each].reshape(QUARTERS, lines, 3, in_each)
    my_in_bias = pick(in_part, quarter, 0).transpose(1, 0, 2).reshape(-1)
    my_up_bias = pick(small[:, 4 * each + 3 * in_each :].reshape(QUARTERS, -1), quarter, 0)

    sequence = gather_team(tokens)
    rows_here = in_weight.shape[1]
    block_in = in_weight.transpose(1, 0, 2).reshape(rows_here, 3, QUARTERS, -1)
    block_in = block_in.transpose(0, 2, 1, 3).reshape(rows_here, QUARTERS, -1)
    full_in = gather_weight(block_in)
    full_out = gather_weight(out_weight.reshape(rows_here, QUARTERS, -1))
    full_up = gather_weight(up_weight.reshape(rows_here, QUARTERS, -1))
    full_down = gather_weight(down_weight.reshape(rows_here, QUARTERS, -1))
    grad_rows = gather_team(cotangent)

    group_rows = sequence.shape[0]
    length = n_mp * own_rows
    groups = group_rows // length
    unit_rows = normalize(sequence.astype(F32))[0]
    normed = (unit_rows * full_gain + full_shift).astype(BF16)
    projected = jnp.dot(normed, full_in, preferred_element_type=F32) + my_in_bias
    heads_here = projected.shape[1] // (3 * HEAD)
    projected = projected.reshape(groups, length, 3, heads_here, HEAD)
    cosine, sine = rotary_tables(length)
    query_pre = projected[:, :, 0]
    key_pre = projected[:, :, 1]
    queries = rotate(query_pre, cosine, sine).astype(BF16)
    keys = rotate(key_pre, cosine, sine).astype(BF16)
    values = projected[:, :, 2].astype(BF16)
    probs = attend(queries, keys)
    probs_low = probs.astype(BF16)
    mixed = jnp.einsum("ghqk,gkhe->gqhe", probs_low, values, preferred_element_type=F32)
    mixed = mixed.reshape(group_rows, heads_here * HEAD).astype(BF16)

    grad_out = jnp.einsum("sd,se->de", grad_rows, mixed, preferred_element_type=F32)
    own_grad_out = scatter_grad(grad_out)
    grad_mixed = jnp.dot(grad_rows, full_out, preferred_element_type=F32).astype(BF16)
    grad_mixed = grad_mixed.reshape(groups, length, heads_here, HEAD)
    grad_probs = jnp.einsum("gqhe,gkhe->ghqk", grad_mixed, values, preferred_element_type=F32)
    row_total = jnp.sum(probs * grad_probs, axis=-1, keepdims=True)
    grad_scores = (probs * (grad_probs - row_total)).astype(BF16)
    grad_values = jnp.einsum(
        "ghqk,gqhe->gkhe", probs_low, grad_mixed, preferred_element_type=F32
    ).astype(BF16)
    score_scale = 1.0 / math.sqrt(HEAD)
    grad_queries = (
        jnp.einsum("ghqk,gkhe->gqhe", grad_scores, keys, preferred_element_type=F32) * score_scale
    ).astype(BF16)
    grad_keys = (
        jnp.einsum("ghqk,gqhe->gkhe", grad_scores, queries, preferred_element_type=F32)
        * score_scale
    ).astype(BF16)

    def turn(vectors):
        return rotate(vectors, cosine, sine)

    turn_pull = jax.vjp(turn, query_pre)[1]
    query_back = turn_pull(grad_queries.astype(F32))[0].astype(BF16)
    key_back = turn_pull(grad_keys.astype(F32))[0].astype(BF16)
    grad_proj = jnp.stack([query_back, key_back, grad_values], axis=2).reshape(group_rows, -1)
    grad_in = jnp.einsum("sd,se->de", normed, grad_proj, preferred_element_type=F32)
    own_grad_in = scatter_grad(grad_in)
    grad_in_bias = jnp.sum(grad_proj.astype(F32), axis=0)

    preact = jnp.dot(normed, full_up, preferred_element_type=F32) + my_up_bias
    activated = smooth_gate(preact).astype(BF16)
    grad_down = jnp.einsum("sd,sf->df", grad_rows, activated, preferred_element_type=F32)
    own_grad_down = scatter_grad(grad_down)
    grad_act = jnp.dot(grad_rows, full_down, preferred_element_type=F32)
    gate_pull = jax.vjp(smooth_gate, preact)[1]
    grad_pre = gate_pull(grad_act)[0].astype(BF16)
    grad_up = jnp.einsum("sd,sf->df", normed, grad_pre, preferred_element_type=F32)
    own_grad_up = scatter_grad(grad_up)
    grad_up_bias = jnp.sum(grad_pre.astype(F32), axis=0)

    branches = jnp.einsum("se,de->sd", mixed, full_out, preferred_element_type=F32)
    branches = branches + jnp.einsum("sf,df->sd", activated, full_down, preferred_element_type=F32)
    summed = scatter_team(branches)
    outcome = (tokens.astype(F32) + summed + full_out_bias + full_down_bias).astype(BF16)

    grad_normed = jnp.einsum("sf,df->sd", grad_pre, full_up, preferred_element_type=F32)
    grad_normed = grad_normed + jnp.einsum(
        "se,de->sd", grad_proj, full_in, preferred_element_type=F32
    )
    grad_own = scatter_team(grad_normed)
    own_unit, own_inv = normalize(tokens.astype(F32))
    gain_part = jnp.sum(grad_own * own_unit, axis=0)
    shift_part = jnp.sum(grad_own, axis=0)
    bias_part = jnp.sum(cotangent.astype(F32), axis=0)
    scaled = grad_own * full_gain
    centered_grad = (
        scaled
        - jnp.mean(scaled, axis=-1, keepdims=True)
        - own_unit * jnp.mean(scaled * own_unit, axis=-1, keepdims=True)
    )
    grad_input = cotangent.astype(F32) + own_inv * centered_grad

    wide = jnp.stack([gain_part, shift_part, bias_part])
    wide = lax.psum(wide, "mp").reshape(3, n_dp, each).transpose(1, 0, 2).reshape(n_dp, 3 * each)
    in_blocks = grad_in_bias.reshape(3, lines, in_each).transpose(1, 0, 2).reshape(lines, -1)
    up_blocks = grad_up_bias.reshape(lines, up_each)
    mine = jnp.concatenate([in_blocks, up_blocks], axis=1)
    spread = place(jnp.zeros((QUARTERS,) + mine.shape, F32), mine, quarter, 0)
    vector = jnp.concatenate([wide, spread.reshape(n_dp, -1)], axis=1)
    owned = lax.psum_scatter(vector, "dp", scatter_dimension=0, tiled=True).reshape(-1)
    own_gain = owned[:each]
    own_shift = owned[each : 2 * each]
    own_bias = owned[2 * each : 3 * each]
    own_in_bias = owned[3 * each : 3 * each + 3 * in_each].reshape(3, in_each)
    own_up_bias = owned[3 * each + 3 * in_each :]

    final_in = own_grad_in.reshape(rows_here, QUARTERS, 3, -1).transpose(2, 0, 1, 3)
    return (
        outcome,
        grad_input,
        own_gain,
        own_shift,
        final_in.reshape(in_weight.shape),
        own_in_bias,
        own_grad_out.reshape(out_weight.shape),
        own_bias,
        own_grad_up.reshape(up_weight.shape),
        own_up_bias,
        own_grad_down.reshape(down_weight.shape),
        own_bias,
    )


def solution(mesh):
    return jax.shard_map(
        per_device,
        mesh=mesh,
        in_specs=(
            P(("dp", "mp"), None),
            P("dp"),
            P("dp"),
            P(None, "dp", "mp"),
            P(None, ("mp", "dp")),
            P("dp", "mp"),
            P("dp"),
            P("dp", "mp"),
            P(("mp", "dp")),
            P("dp", "mp"),
            P("dp"),
            P(("dp", "mp"), None),
        ),
        out_specs=(
            P(("dp", "mp"), None),
            P(("dp", "mp"), None),
            P("dp"),
            P("dp"),
            P(None, "dp", "mp"),
            P(None, ("mp", "dp")),
            P("dp", "mp"),
            P("dp"),
            P("dp", "mp"),
            P(("mp", "dp")),
            P("dp", "mp"),
            P("dp"),
        ),
        check_vma=False,
    )
```

```python
import functools
import math

import jax
import jax.numpy as jnp
from jax import lax
from jax.experimental import pallas as pl
from jax.experimental.pallas import tpu as pltpu
from jax.sharding import PartitionSpec as P

HEAD = 64
ROT = 32
QUARTERS = 4
SMALL = 16
norm_eps = 1e-05
F32 = jnp.float32
BF16 = jnp.bfloat16


def normalize(rows):
    middle = jnp.mean(rows, axis=-1, keepdims=True)
    centered = rows - middle
    spread = jnp.mean(centered * centered, axis=-1, keepdims=True)
    inv_spread = lax.rsqrt(spread + norm_eps)
    return (centered * inv_spread, inv_spread)


def attention_kernel(heads, pre_ref, table_ref, dout_ref, mixed_ref, back_ref):
    length, wide = dout_ref.shape
    block = length // 2
    half_rot = ROT // 2
    scale = 1.0 / math.sqrt(HEAD)
    cosine, first, second = table_ref[0], table_ref[1], table_ref[2]

    def turn(v):
        return (
            v * cosine
            + pltpu.roll(v, wide - half_rot, 1) * first
            + pltpu.roll(v, half_rot, 1) * second
        )

    def turn_back(g):
        return (
            g * cosine
            + pltpu.roll(g * first, half_rot, 1)
            + pltpu.roll(g * second, wide - half_rot, 1)
        )

    queries = turn(pre_ref[0]).astype(BF16)
    keys = turn(pre_ref[1]).astype(BF16)
    values = pre_ref[2].astype(BF16)
    douts = dout_ref[...]
    head_of = lax.broadcasted_iota(jnp.int32, (block, wide), 1) // HEAD
    nothing = jnp.zeros((block, wide), BF16)
    mixed = [None, None]
    dq, dk, dv = [None, None], [None, None], [None, None]

    def dot(a, b, contract):
        return lax.dot_general(a, b, (contract, ((), ())), preferred_element_type=F32)

    def add(total, part):
        return part if total is None else total + part

    for head in range(heads):
        here = head_of == head

        def only(v):
            return jnp.where(here, v, nothing)

        q_here = [only(queries[i * block : (i + 1) * block]) for i in range(2)]
        k_here = [only(keys[i * block : (i + 1) * block]) for i in range(2)]
        v_here = [only(values[i * block : (i + 1) * block]) for i in range(2)]
        d_here = [only(douts[i * block : (i + 1) * block]) for i in range(2)]
        for i in range(2):
            seen = (i + 1) * block
            scores = dot(q_here[i], keys[:seen], ((1,), (1,))) * scale
            row = lax.broadcasted_iota(jnp.int32, (block, seen), 0) + i * block
            col = lax.broadcasted_iota(jnp.int32, (block, seen), 1)
            scores = jnp.where(col <= row, scores, -1e30)
            powers = jnp.exp(scores - jnp.max(scores, axis=1, keepdims=True))
            probs = powers * (1.0 / jnp.sum(powers, axis=1, keepdims=True))
            low = probs.astype(BF16)
            dprobs = dot(d_here[i], values[:seen], ((1,), (1,)))
            total = jnp.sum(probs * dprobs, axis=1, keepdims=True)
            dscores = (probs * (dprobs - total)).astype(BF16)
            for j in range(i + 1):
                part = slice(j * block, (j + 1) * block)
                mixed[i] = add(mixed[i], dot(low[:, part], v_here[j], ((1,), (0,))))
                dq[i] = add(dq[i], dot(dscores[:, part], k_here[j], ((1,), (0,))))
                dv[j] = add(dv[j], dot(low[:, part], d_here[i], ((0,), (0,))))
                dk[j] = add(dk[j], dot(dscores[:, part], q_here[i], ((0,), (0,))))
    mixed_ref[...] = jnp.concatenate(mixed, axis=0).astype(BF16)
    dq_low = (jnp.concatenate(dq, axis=0) * scale).astype(BF16)
    dk_low = (jnp.concatenate(dk, axis=0) * scale).astype(BF16)
    back_ref[0] = turn_back(dq_low.astype(F32)).astype(BF16)
    back_ref[1] = turn_back(dk_low.astype(F32)).astype(BF16)
    back_ref[2] = jnp.concatenate(dv, axis=0).astype(BF16)


def rotary_tables(length, heads):
    half_rot = ROT // 2
    position = jnp.arange(length, dtype=F32)
    freqs = jnp.exp(jnp.arange(half_rot, dtype=F32) * (-math.log(10000.0) / half_rot))
    angles = position[:, None] * freqs[None, :]
    cosine, sine = jnp.cos(angles), jnp.sin(angles)
    rest = jnp.zeros((length, HEAD - ROT), F32)
    none = jnp.zeros_like(sine)
    tables = jnp.stack(
        [
            jnp.concatenate([cosine, cosine, rest + 1.0], axis=1),
            jnp.concatenate([-sine, none, rest], axis=1),
            jnp.concatenate([none, sine, rest], axis=1),
        ]
    )
    return jnp.tile(tables, (1, 1, heads))


def attention(projected, tables, grad_mixed):
    _, length, wide = tables.shape
    rows = grad_mixed.shape[0]
    heads = wide // HEAD
    pairs = rows // length * heads
    return pl.pallas_call(
        functools.partial(attention_kernel, heads),
        grid=(rows // length,),
        out_shape=(
            jax.ShapeDtypeStruct((rows, wide), BF16),
            jax.ShapeDtypeStruct((3, rows, wide), BF16),
        ),
        in_specs=[
            pl.BlockSpec((3, length, wide), lambda g: (0, g, 0)),
            pl.BlockSpec((3, length, wide), lambda g: (0, 0, 0)),
            pl.BlockSpec((length, wide), lambda g: (g, 0)),
        ],
        out_specs=(
            pl.BlockSpec((length, wide), lambda g: (g, 0)),
            pl.BlockSpec((3, length, wide), lambda g: (0, g, 0)),
        ),
        compiler_params=pltpu.CompilerParams(vmem_limit_bytes=40 * 2**20),
        cost_estimate=pl.CostEstimate(
            flops=14 * pairs * length * length * HEAD,
            bytes_accessed=24 * rows * wide,
            transcendentals=pairs * length * length,
        ),
    )(projected, tables, grad_mixed)


MESH = pl.DeviceIdType.MESH


def gather_kernel(
    lines,
    tok_ref,
    cot_ref,
    in_ref,
    out_ref,
    up_ref,
    small_ref,
    seq_ref,
    grad_ref,
    heads_ref,
    up_full_ref,
    smalls_ref,
    local_sem,
    swap_send,
    swap_recv,
    team_send,
    team_recv,
    line_send,
    line_recv,
):
    dp = lax.axis_index("dp")
    mp = lax.axis_index("mp")
    quarter = dp % QUARTERS
    line = dp // QUARTERS
    other = 1 - mp
    rows = tok_ref.shape[0]
    depth = out_ref.shape[0]
    wide = out_ref.shape[1] // QUARTERS
    tall = small_ref.shape[0]
    up_wide = up_ref.shape[1] // QUARTERS

    barrier = pltpu.get_barrier_semaphore()
    for peer in ((dp ^ 1, mp), (dp ^ 2, mp), (dp ^ 3, mp), (dp, other)):
        pl.semaphore_signal(barrier, inc=1, device_id=peer, device_id_type=MESH)
    has_above = line < lines - 1
    has_below = line > 0

    @pl.when(has_above)
    def _():
        pl.semaphore_signal(barrier, inc=1, device_id=(dp + QUARTERS, mp), device_id_type=MESH)

    @pl.when(has_below)
    def _():
        pl.semaphore_signal(barrier, inc=1, device_id=(dp - QUARTERS, mp), device_id_type=MESH)

    pl.semaphore_wait(barrier, 4 + has_above.astype(jnp.int32) + has_below.astype(jnp.int32))

    def columns(index, size):
        return pl.ds(pl.multiple_of(index * size, size), size)

    def weight_views(device, to):
        part = columns(device % QUARTERS, depth)
        return (
            (small_ref, smalls_ref.at[columns(device, tall), :]),
            (up_ref.at[:, columns(to, up_wide)], up_full_ref.at[columns(device, depth), :]),
            (in_ref.at[:, :, columns(to, wide)], heads_ref.at[0:3, part, :]),
            (out_ref.at[:, columns(to, wide)], heads_ref.at[3, part, :]),
        )

    def swap(kind, j, device):
        src, dst = weight_views(device, quarter ^ j)[kind]
        return pltpu.make_async_remote_copy(
            src_ref=src,
            dst_ref=dst,
            send_sem=swap_send.at[kind, j - 1],
            recv_sem=swap_recv.at[kind, j - 1],
            device_id=(dp ^ j, mp),
            device_id_type=MESH,
        )

    def seat(device, half_of):
        return columns((device % QUARTERS) * 2 + half_of, rows)

    rows_of = ((tok_ref, seq_ref), (cot_ref, grad_ref))

    def relay(which, number, place, peer):
        view = rows_of[which][1].at[place, :]
        return pltpu.make_async_remote_copy(
            src_ref=view,
            dst_ref=view,
            send_sem=team_send.at[which, number],
            recv_sem=team_recv.at[which, number],
            device_id=peer,
            device_id_type=MESH,
        )

    def offer(which, number, peer):
        src, dst = rows_of[which]
        return pltpu.make_async_remote_copy(
            src_ref=src,
            dst_ref=dst.at[seat(dp, mp), :],
            send_sem=team_send.at[which, number],
            recv_sem=team_recv.at[which, number],
            device_id=peer,
            device_id_type=MESH,
        )

    across, aside, twin = (dp ^ 2, mp), (dp, other), (dp ^ 1, mp)

    def part_seat(device, half_of, part):
        low = rows // 4 * 3
        start = ((device % QUARTERS) * 2 + half_of) * rows + part * low
        size = rows - low if part else low
        return pl.ds(pl.multiple_of(start, rows // 4), size)

    def line_views(kind, chunk):
        if kind == 0:
            return smalls_ref.at[columns(chunk, QUARTERS * tall), :]
        return up_full_ref.at[columns(chunk, QUARTERS * depth), :]

    def line_copy(kind, way, step, chunk):
        view = line_views(kind, chunk)
        return pltpu.make_async_remote_copy(
            src_ref=view,
            dst_ref=view,
            send_sem=line_send.at[kind, way, step - 1],
            recv_sem=line_recv.at[kind, way, step - 1],
            device_id=(dp + (QUARTERS if way == 0 else -QUARTERS), mp),
            device_id_type=MESH,
        )

    def sends(way, step):
        if way == 0:
            return (line >= step - 1) & has_above, line - (step - 1)
        return (line <= lines - step) & has_below, line + (step - 1)

    def takes(way, step):
        if way == 0:
            return line >= step, line - step
        return line <= lines - 1 - step, line + step

    def start_line(kinds, step):
        for kind in kinds:
            for way in (0, 1):
                go, chunk = sends(way, step)

                @pl.when(go)
                def _():
                    line_copy(kind, way, step, chunk).start()

    def wait_line(kinds, step):
        for kind in kinds:
            for way in (0, 1):
                go, chunk = takes(way, step)

                @pl.when(go)
                def _():
                    line_copy(kind, way, step, chunk).wait_recv()

    own = []
    for kind, (src, dst) in enumerate(weight_views(dp, quarter)):
        own.append(pltpu.make_async_copy(src, dst, local_sem.at[kind]))
    for which, (src, dst) in enumerate(rows_of):
        own.append(
            pltpu.make_async_copy(src, dst.at[seat(dp, mp), :], local_sem.at[4 + which])
        )
    pending = []

    def begin(*copies):
        for copy in copies:
            copy.start()
            pending.append(copy)

    near, beside = seat(dp ^ 2, mp), seat(dp, other)

    def pass_on(which):
        relay(which, 0, near, across).wait_recv()
        begin(
            relay(which, 3, part_seat(dp ^ 2, mp, 0), aside),
            relay(which, 4, near, twin),
        )
        relay(which, 1, beside, aside).wait_recv()
        begin(
            relay(which, 5, part_seat(dp, other, 1), across),
            relay(which, 6, beside, twin),
        )

    def hand_over(which):
        for part, peer in ((0, aside), (1, across)):
            far = part_seat(dp ^ 2, other, part)
            relay(which, 3 + 2 * part, far, peer).wait_recv()
            begin(relay(which, 7 + part, far, twin))

    for kind in (0, 1):
        begin(*[swap(kind, j, dp) for j in (2, 3, 1)])
        own[kind].start()
    begin(offer(0, 1, aside), offer(0, 2, twin))
    for kind in (2, 3, 4, 5):
        own[kind].start()
    for kind in (0, 1):
        own[kind].wait()
        for j in (1, 2, 3):
            swap(kind, j, dp ^ j).wait_recv()
    if lines > 1:
        start_line((0, 1), 1)
    begin(offer(0, 0, across), offer(1, 1, aside), offer(1, 2, twin))

    def tokens_round():
        pass_on(0)
        begin(offer(1, 0, across))
        hand_over(0)

    def grads_round():
        pass_on(1)
        for kind in (2, 3):
            begin(*[swap(kind, j, dp) for j in (2, 3, 1)])

    rounds = [tokens_round, grads_round]
    for step in range(1, lines):
        wait_line((0, 1), step)
        if step < lines - 1:
            start_line((0, 1), step + 1)
        if rounds:
            rounds.pop(0)()
    for left in rounds:
        left()
    hand_over(1)

    for number in (2, 3, 4, 5):
        own[number].wait()
    for kind in (2, 3):
        for j in (1, 2, 3):
            swap(kind, j, dp ^ j).wait_recv()
    for which in (0, 1):
        relay(which, 2, seat(dp ^ 1, mp), twin).wait_recv()
        relay(which, 4, seat(dp ^ 3, mp), twin).wait_recv()
        relay(which, 6, seat(dp ^ 1, other), twin).wait_recv()
        for part in (0, 1):
            relay(which, 7 + part, part_seat(dp ^ 3, other, part), twin).wait_recv()
    for copy in pending:
        copy.wait_send()
    for kind in (0, 1):
        for step in range(1, lines):
            for way in (0, 1):
                go, chunk = sends(way, step)

                @pl.when(go)
                def _():
                    line_copy(kind, way, step, chunk).wait_send()


def gather_first(lines, team, tokens, cotangent, in_weight, out_weight, up_weight, small):
    depth = out_weight.shape[0]
    wide = out_weight.shape[1] // QUARTERS
    up_wide = up_weight.shape[1] // QUARTERS
    whole = lines * QUARTERS * depth
    anywhere = pl.BlockSpec(memory_space=pl.ANY)
    steps = max(lines - 1, 1)
    together = jax.ShapeDtypeStruct((team * tokens.shape[0], tokens.shape[1]), BF16)
    return pl.pallas_call(
        functools.partial(gather_kernel, lines),
        out_shape=(
            together,
            together,
            jax.ShapeDtypeStruct((4, QUARTERS * depth, wide), BF16),
            jax.ShapeDtypeStruct((whole, up_wide), BF16),
            jax.ShapeDtypeStruct((lines * QUARTERS * small.shape[0], small.shape[1]), BF16),
        ),
        in_specs=[anywhere] * 6,
        out_specs=(anywhere,) * 5,
        scratch_shapes=[
            pltpu.SemaphoreType.DMA((6,)),
            pltpu.SemaphoreType.DMA((4, 3)),
            pltpu.SemaphoreType.DMA((4, 3)),
            pltpu.SemaphoreType.DMA((2, 9)),
            pltpu.SemaphoreType.DMA((2, 9)),
            pltpu.SemaphoreType.DMA((2, 2, steps)),
            pltpu.SemaphoreType.DMA((2, 2, steps)),
        ],
        compiler_params=pltpu.CompilerParams(collective_id=1, has_side_effects=True),
    )(tokens, cotangent, in_weight, out_weight, up_weight, small)


def small_kernel(lines, both, vec_ref, total_ref, land_a, part, land_b, land_c, send, recv):
    dp = lax.axis_index("dp")
    mp = lax.axis_index("mp")
    quarter = dp % QUARTERS
    line = dp // QUARTERS
    aside = (dp, 1 - mp)

    def in_line(k):
        return (lax.rem(line + k, lines) * QUARTERS + quarter, mp)

    barrier = pltpu.get_barrier_semaphore()
    peers = [(dp ^ j, mp) for j in (1, 2, 3)] + [in_line(k) for k in range(1, lines)] + [aside]
    for peer in peers:
        pl.semaphore_signal(barrier, inc=1, device_id=peer, device_id_type=MESH)
    pl.semaphore_wait(barrier, len(peers))

    def move(number, src, dst, peer):
        return pltpu.make_async_remote_copy(
            src_ref=src,
            dst_ref=dst,
            send_sem=send.at[number],
            recv_sem=recv.at[number],
            device_id=peer,
            device_id_type=MESH,
        )

    first = [
        move(j - 1, vec_ref.at[quarter ^ j], land_a.at[j - 1], (dp ^ j, mp)) for j in (1, 2, 3)
    ]
    for copy in first:
        copy.start()
    for copy in first:
        copy.wait()
    part[...] = (vec_ref[quarter] + land_a[0]) + (land_a[1] + land_a[2])
    second = [
        move(2 + k, part.at[lax.rem(line + k, lines)], land_b.at[k - 1], in_line(k))
        for k in range(1, lines)
    ]
    for copy in second:
        copy.start()
    total = part[line]
    for k, copy in enumerate(second):
        copy.wait()
        total = total + land_b[k]
    total_ref[...] = total
    third = move(2 + lines, total_ref, land_c, aside)
    third.start()
    third.wait()
    shape = total_ref.shape
    index = lax.broadcasted_iota(jnp.int32, shape, 0) * shape[1]
    index = index + lax.broadcasted_iota(jnp.int32, shape, 1)
    total_ref[...] = jnp.where(index < both, total + land_c[...], total)


def sum_small(lines, both, vector):
    tile = vector.shape[2:]
    count = lines + 3
    return pl.pallas_call(
        functools.partial(small_kernel, lines, both),
        out_shape=jax.ShapeDtypeStruct(tile, F32),
        in_specs=[pl.BlockSpec(memory_space=pltpu.VMEM)],
        out_specs=pl.BlockSpec(memory_space=pltpu.VMEM),
        scratch_shapes=[
            pltpu.VMEM((3, lines) + tile, F32),
            pltpu.VMEM((lines,) + tile, F32),
            pltpu.VMEM((max(lines - 1, 1),) + tile, F32),
            pltpu.VMEM(tile, F32),
            pltpu.SemaphoreType.DMA((count,)),
            pltpu.SemaphoreType.DMA((count,)),
        ],
        compiler_params=pltpu.CompilerParams(collective_id=2, has_side_effects=True),
    )(vector)


def smooth_gate(u):
    slope = math.sqrt(2.0 / math.pi)
    square = u * u
    curve = jnp.tanh(slope * (u + 0.044715 * (u * square)))
    rise = 0.5 * (1.0 + curve)
    bend = 0.5 * u * (1.0 - curve * curve) * (slope * (1.0 + 3.0 * 0.044715 * square))
    return u * rise, rise + bend


def norm_kernel(rows_ref, gain_ref, shift_ref, out_ref):
    rows = rows_ref[...].astype(F32)
    unit = normalize(rows)[0]
    out_ref[...] = (unit * gain_ref[...] + shift_ref[...]).astype(BF16)


def norm_rows(rows, gain, shift):
    count, width = rows.shape
    block = min(count, 256)
    return pl.pallas_call(
        norm_kernel,
        grid=(count // block,),
        out_shape=jax.ShapeDtypeStruct((count, width), BF16),
        in_specs=[
            pl.BlockSpec((block, width), lambda i: (i, 0)),
            pl.BlockSpec((1, width), lambda i: (0, 0)),
            pl.BlockSpec((1, width), lambda i: (0, 0)),
        ],
        out_specs=pl.BlockSpec((block, width), lambda i: (i, 0)),
        cost_estimate=pl.CostEstimate(
            flops=8 * count * width, bytes_accessed=4 * count * width, transcendentals=0
        ),
    )(rows, gain, shift)


def per_device(
    tokens,
    norm_gain,
    norm_shift,
    in_weight,
    in_bias,
    out_weight,
    out_bias,
    up_weight,
    up_bias,
    down_weight,
    down_bias,
    cotangent,
):
    n_dp = lax.axis_size("dp")
    n_mp = lax.axis_size("mp")
    lines = n_dp // QUARTERS
    dp = lax.axis_index("dp")
    mp = lax.axis_index("mp")
    quarter = dp % QUARTERS
    line = dp // QUARTERS
    team = QUARTERS * n_mp
    own_rows, width = tokens.shape

    last = [None]

    def then(*values):
        if last[0] is not None:
            *values, last[0] = lax.optimization_barrier(values + (last[0],))
        return values if len(values) > 1 else values[0]

    def ended(value):
        last[0] = value
        return value

    def pick(array, index, axis):
        return lax.dynamic_index_in_dim(array, index, axis, keepdims=False)

    def place(buffer, piece, index, axis):
        return lax.dynamic_update_index_in_dim(buffer, piece, index, axis)

    def swap_quarters(array, axis):
        got = []
        for j in range(QUARTERS):
            piece = pick(array, quarter ^ j, axis)
            if j:
                piece = lax.ppermute(piece, "dp", [(d, d ^ j) for d in range(n_dp)])
            got.append(piece)
        return got

    class Lines:
        def __init__(self, piece):
            self.ups, self.downs = [piece], [piece]

        def step(self):
            k = len(self.ups)
            if k < lines:
                up_pairs = [
                    (d, d + QUARTERS)
                    for d in range(n_dp)
                    if k - 1 <= d // QUARTERS < lines - 1
                ]
                down_pairs = [(n_dp - 1 - a, n_dp - 1 - b) for a, b in up_pairs]
                self.ups.append(lax.ppermute(self.ups[-1], "dp", up_pairs))
                self.downs.append(lax.ppermute(self.downs[-1], "dp", down_pairs))

        def meet(self):
            if len(self.ups) > 1:
                self.ups[-1], self.downs[-1] = then(self.ups[-1], self.downs[-1])
                ended(self.ups[-1])
                ended(self.downs[-1])

        def whole(self, axis):
            while len(self.ups) < lines:
                self.step()
            self.meet()
            slots = []
            for slot in range(lines):
                case = [
                    self.ups[k - slot] if k >= slot else self.downs[slot - k]
                    for k in range(lines)
                ]
                slots.append(lax.select_n(jnp.broadcast_to(line, case[0].shape), *case))
            return jnp.concatenate(slots, axis=axis)

    def in_order(got):
        which = jnp.broadcast_to(quarter, got[0].shape)
        return [
            lax.select_n(which, *[got[k ^ slot] for k in range(QUARTERS)])
            for slot in range(QUARTERS)
        ]

    def swap_rows(block):
        return jnp.concatenate(in_order(swap_quarters(block, 1)), axis=0)

    class Sums:
        def __init__(self, chunk):
            self.chunk = chunk
            self.ups, self.downs = [], []

        def add(self, index, got):
            part = self.chunk(jnp.clip(index, 0, lines - 1))
            if not got:
                return part.astype(BF16)
            return (part.astype(F32) + got[-1].astype(F32)).astype(BF16)

        def step(self):
            k = len(self.ups) + 1
            if k < lines:
                up_pairs = [
                    (d, d + QUARTERS)
                    for d in range(n_dp)
                    if d // QUARTERS <= min(k - 1, lines - 2)
                ]
                down_pairs = [(n_dp - 1 - a, n_dp - 1 - b) for a, b in up_pairs]
                up = self.add(line + (lines - k), self.ups)
                down = self.add(line - (lines - k), self.downs)
                self.ups.append(lax.ppermute(up, "dp", up_pairs))
                self.downs.append(lax.ppermute(down, "dp", down_pairs))

        def meet(self):
            if self.ups:
                self.ups[-1], self.downs[-1] = then(self.ups[-1], self.downs[-1])
                ended(self.downs[-1])

        def total(self):
            while len(self.ups) < lines - 1:
                self.meet()
                self.step()
            self.meet()
            part = self.chunk(line).astype(F32)
            return (part + self.ups[-1].astype(F32) + self.downs[-1].astype(F32)).astype(BF16)

    def hand_out(total, axis):
        shape = total.shape
        got = swap_quarters(total.reshape(shape[:axis] + (QUARTERS, -1) + shape[-1:]), axis)
        return jnp.concatenate([piece.astype(F32) for piece in in_order(got)], axis=axis + 1)

    def chunk_of(grad, axis):
        size = grad.shape[axis] // lines

        def chunk(index):
            return lax.dynamic_slice_in_dim(grad, index * size, size, axis)

        return chunk

    core = dp % 2
    half = (dp // 2) % (QUARTERS // 2)

    def of_core(array, which):
        parts = array.reshape((QUARTERS // 2, 2, n_mp * own_rows) + array.shape[1:])
        return pick(parts, which, 1).reshape((-1,) + array.shape[1:])

    def to_twin(rows):
        return lax.ppermute(rows, "dp", [(d, d ^ 1) for d in range(n_dp)])

    def to_owners(pair):
        pair = pair.reshape(QUARTERS // 2, n_mp, own_rows, width)
        parts = []
        for a in range(QUARTERS // 2):
            for b in range(n_mp):
                piece = pick(pick(pair, half ^ a, 0), (mp + b) % n_mp, 0)
                if a or b:
                    pairs = [
                        (d * n_mp + m, (d ^ (2 * a)) * n_mp + (m + b) % n_mp)
                        for d in range(n_dp)
                        for m in range(n_mp)
                    ]
                    piece = lax.ppermute(piece, ("dp", "mp"), pairs)
                parts.append(piece)
        return parts

    def add_up(parts):
        return sum(part.astype(F32) for part in parts)

    small = jnp.concatenate(
        [norm_gain, norm_shift, out_bias, down_bias, in_bias.reshape(-1), up_bias]
    )
    small = jnp.pad(small, (0, SMALL * 128 - small.shape[0])).reshape(SMALL, 128)
    sequence, grad_rows, heads_part, full_up, small = gather_first(
        lines, team, tokens, cotangent, in_weight, out_weight, up_weight, small
    )
    small = small.reshape(n_dp, -1).astype(F32)
    each = norm_gain.shape[0]
    full_gain = small[:, :each].reshape(-1)
    full_shift = small[:, each : 2 * each].reshape(-1)
    full_out_bias = small[:, 2 * each : 3 * each].reshape(-1)
    full_down_bias = small[:, 3 * each : 4 * each].reshape(-1)
    in_each = in_bias.shape[1]
    up_each = up_bias.shape[0]
    in_part = small[:, 4 * each : 4 * each + 3 * in_each].reshape(QUARTERS, lines, 3, in_each)
    my_in_bias = pick(in_part, quarter, 0).transpose(1, 0, 2).reshape(3, 1, -1)
    ends = 4 * each + 3 * in_each
    my_up_bias = pick(small[:, ends : ends + up_each].reshape(QUARTERS, -1), quarter, 0)

    rows_here = in_weight.shape[1]
    ended(sequence)
    heads_lines = Lines(heads_part)
    heads_lines.step()
    down_block = then(down_weight.reshape(rows_here, QUARTERS, -1))
    down_part = swap_rows(down_block)

    length = n_mp * own_rows
    normed = norm_rows(sequence, full_gain.reshape(1, -1), full_shift.reshape(1, -1))
    ended(normed)
    heads_lines.meet()
    heads_lines.step()
    preact = jnp.dot(normed, full_up, preferred_element_type=F32) + my_up_bias
    activated, slope = smooth_gate(preact)
    activated, slope = lax.optimization_barrier((activated.astype(BF16), slope.astype(BF16)))
    ended(activated)
    grad_down = jnp.einsum(
        "sd,sf->df", then(grad_rows), activated, preferred_element_type=F32
    ).astype(BF16)
    ended(grad_down)
    down_sums = Sums(chunk_of(grad_down, 0))
    down_sums.step()
    heads_lines.meet()
    heads_lines.step()
    down_part = ended(then(down_part))
    heads_lines.meet()
    down_lines = Lines(then(down_part))
    down_lines.step()
    down_sums.meet()
    down_sums.step()

    full_heads = heads_lines.whole(1)
    full_in, full_out = full_heads[:3], full_heads[3]
    projected = (
        jnp.einsum("sd,kde->kse", then(normed), full_in, preferred_element_type=F32) + my_in_bias
    )
    ended(projected)
    grad_mixed = jnp.dot(
        then(grad_rows), full_out, preferred_element_type=F32
    ).astype(BF16)
    ended(grad_mixed)
    down_lines.meet()
    down_lines.step()
    down_sums.meet()
    down_sums.step()
    tables = rotary_tables(length, projected.shape[2] // HEAD)
    mixed, grad_proj = attention(then(projected), tables, grad_mixed)
    ended(grad_proj)
    down_lines.meet()
    down_lines.step()
    grad_out = jnp.einsum(
        "sd,se->de", then(grad_rows), mixed, preferred_element_type=F32
    ).astype(BF16)
    ended(grad_out)
    grad_in = jnp.einsum(
        "sd,kse->kde", then(normed), grad_proj, preferred_element_type=F32
    ).astype(BF16)
    ended(grad_in)
    in_chunk, out_chunk = chunk_of(grad_in, 1), chunk_of(grad_out, 0)
    heads_sums = Sums(lambda k: jnp.concatenate([in_chunk(k), out_chunk(k)[None]], axis=0))
    heads_sums.step()
    grad_in_bias = jnp.sum(grad_proj.astype(F32), axis=1)
    down_sums.meet()
    own_grad_down = hand_out(down_sums.total(), 0)

    full_down = ended(down_lines.whole(0))
    grad_act = jnp.dot(then(grad_rows), full_down, preferred_element_type=F32)
    grad_pre = ended((grad_act * slope.astype(F32)).astype(BF16))
    heads_sums.meet()
    heads_sums.step()
    grad_up = jnp.einsum(
        "sd,sf->df", then(normed), grad_pre, preferred_element_type=F32
    ).astype(BF16)
    ended(grad_up)
    up_sums = Sums(chunk_of(grad_up, 0))
    up_sums.step()
    grad_up_bias = jnp.sum(grad_pre.astype(F32), axis=0)

    def forward_part(which):
        some_mixed, some_act = then(of_core(mixed, which), of_core(activated, which))
        sums = jnp.dot(some_act, full_down.T, preferred_element_type=F32)
        sums = sums + jnp.dot(some_mixed, full_out.T, preferred_element_type=F32)
        return ended(sums.astype(BF16))

    def backward_part(which):
        some_pre, some_proj = then(
            of_core(grad_pre, which), jnp.stack([of_core(grad_proj[k], which) for k in range(3)])
        )
        sums = jnp.dot(some_pre, full_up.T, preferred_element_type=F32)
        sums = sums + jnp.einsum("kse,kde->sd", some_proj, full_in, preferred_element_type=F32)
        return ended(sums.astype(BF16))

    def paired(mine, got):
        mine, got = then(mine, got)
        return ended((mine.astype(F32) + got.astype(F32)).astype(BF16))

    got = to_twin(forward_part(1 - core))
    mine = forward_part(core)
    heads_sums.meet()
    heads_sums.step()
    forward_parts = to_owners(paired(mine, got))
    got = to_twin(backward_part(1 - core))
    up_sums.meet()
    up_sums.step()
    mine = backward_part(core)
    heads_sums.meet()
    own_heads = hand_out(heads_sums.total(), 1)
    own_grad_in, own_grad_out = own_heads[:3], own_heads[3]
    backward_parts = to_owners(paired(mine, got))
    up_sums.meet()
    up_sums.step()
    forward_parts = then(*forward_parts)
    summed = ended(add_up(forward_parts))
    up_sums.meet()
    own_grad_up = hand_out(up_sums.total(), 0)
    outcome = (tokens.astype(F32) + summed + full_out_bias + full_down_bias).astype(BF16)

    grad_own = add_up(backward_parts)
    own_unit, own_inv = normalize(tokens.astype(F32))
    gain_part = jnp.sum(grad_own * own_unit, axis=0)
    shift_part = jnp.sum(grad_own, axis=0)
    bias_part = jnp.sum(cotangent.astype(F32), axis=0)
    scaled = grad_own * full_gain
    centered_grad = (
        scaled
        - jnp.mean(scaled, axis=-1, keepdims=True)
        - own_unit * jnp.mean(scaled * own_unit, axis=-1, keepdims=True)
    )
    grad_input = cotangent.astype(F32) + own_inv * centered_grad

    wide = jnp.stack([gain_part, shift_part, bias_part])
    wide = wide.reshape(3, lines, QUARTERS, each).transpose(2, 1, 0, 3)
    wide = wide.reshape(QUARTERS, lines, 3 * each)
    in_blocks = grad_in_bias.reshape(3, lines, in_each).transpose(1, 0, 2).reshape(lines, -1)
    mine = jnp.concatenate([in_blocks, grad_up_bias.reshape(lines, up_each)], axis=1)
    spread = place(jnp.zeros((QUARTERS,) + mine.shape, F32), mine, quarter, 0)
    spread = spread.reshape(lines, QUARTERS, -1).transpose(1, 0, 2)
    vector = jnp.concatenate([wide, spread], axis=2)
    vector = jnp.pad(vector, ((0, 0), (0, 0), (0, 1024 - vector.shape[2])))
    owned = sum_small(lines, 3 * each, vector.reshape(QUARTERS, lines, 8, 128)).reshape(-1)
    own_gain = owned[:each]
    own_shift = owned[each : 2 * each]
    own_bias = owned[2 * each : 3 * each]
    own_in_bias = owned[3 * each : 3 * each + 3 * in_each].reshape(3, in_each)
    own_up_bias = owned[3 * each + 3 * in_each : 3 * each + 3 * in_each + up_each]

    return (
        outcome,
        grad_input,
        own_gain,
        own_shift,
        own_grad_in.reshape(in_weight.shape),
        own_in_bias,
        own_grad_out.reshape(out_weight.shape),
        own_bias,
        own_grad_up.reshape(up_weight.shape),
        own_up_bias,
        own_grad_down.reshape(down_weight.shape),
        own_bias,
    )


def solution(mesh):
    return jax.shard_map(
        per_device,
        mesh=mesh,
        in_specs=(
            P(("dp", "mp"), None),
            P("dp"),
            P("dp"),
            P(None, "dp", "mp"),
            P(None, ("mp", "dp")),
            P("dp", "mp"),
            P("dp"),
            P("dp", "mp"),
            P(("mp", "dp")),
            P("dp", "mp"),
            P("dp"),
            P(("dp", "mp"), None),
        ),
        out_specs=(
            P(("dp", "mp"), None),
            P(("dp", "mp"), None),
            P("dp"),
            P("dp"),
            P(None, "dp", "mp"),
            P(None, ("mp", "dp")),
            P("dp", "mp"),
            P("dp"),
            P("dp", "mp"),
            P(("mp", "dp")),
            P("dp", "mp"),
            P("dp"),
        ),
        check_vma=False,
    )
```

```python
import functools
import math

import jax
import jax.numpy as jnp
import numpy as np
from jax import lax
from jax.experimental import pallas as pl
from jax.experimental.pallas import tpu as pltpu
from jax.sharding import PartitionSpec as P

HEAD = 64
ROT = 32
QUARTERS = 4
SMALL = 16
norm_eps = 1e-05
F32 = jnp.float32
BF16 = jnp.bfloat16


def normalize(rows):
    middle = jnp.mean(rows, axis=-1, keepdims=True)
    centered = rows - middle
    spread = jnp.mean(centered * centered, axis=-1, keepdims=True)
    inv_spread = lax.rsqrt(spread + norm_eps)
    return (centered * inv_spread, inv_spread)


def roll_lanes(v, by):
    wide = v.shape[1]
    return jnp.concatenate([v[:, wide - by :], v[:, : wide - by]], axis=1)


def attention_block(pre, table, douts):
    length, wide = douts.shape
    heads = wide // HEAD
    block = length // 2
    half_rot = ROT // 2
    scale = 1.0 / math.sqrt(HEAD)
    cosine, first, second = table

    def turn(v):
        return (
            v * cosine
            + roll_lanes(v, wide - half_rot) * first
            + roll_lanes(v, half_rot) * second
        )

    def turn_back(g):
        return (
            g * cosine
            + roll_lanes(g * first, half_rot)
            + roll_lanes(g * second, wide - half_rot)
        )

    queries = turn(pre[0]).astype(BF16)
    keys = turn(pre[1]).astype(BF16)
    values = pre[2].astype(BF16)
    head_of = lax.broadcasted_iota(jnp.int32, (block, wide), 1) // HEAD
    nothing = jnp.zeros((block, wide), BF16)
    mixed = [None, None]
    dq, dk, dv = [None, None], [None, None], [None, None]

    def dot(a, b, contract):
        return lax.dot_general(a, b, (contract, ((), ())), preferred_element_type=F32)

    def add(total, part):
        return part if total is None else total + part

    for head in range(heads):
        here = head_of == head

        def only(v):
            return jnp.where(here, v, nothing)

        q_here = [only(queries[i * block : (i + 1) * block]) for i in range(2)]
        k_here = [only(keys[i * block : (i + 1) * block]) for i in range(2)]
        v_here = [only(values[i * block : (i + 1) * block]) for i in range(2)]
        d_here = [only(douts[i * block : (i + 1) * block]) for i in range(2)]
        for i in range(2):
            seen = (i + 1) * block
            scores = dot(q_here[i], keys[:seen], ((1,), (1,))) * scale
            row = lax.broadcasted_iota(jnp.int32, (block, seen), 0) + i * block
            col = lax.broadcasted_iota(jnp.int32, (block, seen), 1)
            scores = jnp.where(col <= row, scores, -1e30)
            powers = jnp.exp(scores - jnp.max(scores, axis=1, keepdims=True))
            probs = powers * (1.0 / jnp.sum(powers, axis=1, keepdims=True))
            low = probs.astype(BF16)
            dprobs = dot(d_here[i], values[:seen], ((1,), (1,)))
            total = jnp.sum(probs * dprobs, axis=1, keepdims=True)
            dscores = (probs * (dprobs - total)).astype(BF16)
            for j in range(i + 1):
                part = slice(j * block, (j + 1) * block)
                mixed[i] = add(mixed[i], dot(low[:, part], v_here[j], ((1,), (0,))))
                dq[i] = add(dq[i], dot(dscores[:, part], k_here[j], ((1,), (0,))))
                dv[j] = add(dv[j], dot(low[:, part], d_here[i], ((0,), (0,))))
                dk[j] = add(dk[j], dot(dscores[:, part], q_here[i], ((0,), (0,))))
    value = jnp.concatenate(mixed, axis=0).astype(BF16)
    dq_low = (jnp.concatenate(dq, axis=0) * scale).astype(BF16)
    dk_low = (jnp.concatenate(dk, axis=0) * scale).astype(BF16)
    backs = (
        turn_back(dq_low.astype(F32)).astype(BF16),
        turn_back(dk_low.astype(F32)).astype(BF16),
        jnp.concatenate(dv, axis=0).astype(BF16),
    )
    return value, backs


def rotary_tables(length, heads):
    half_rot = ROT // 2
    freqs = np.exp(np.arange(half_rot) * (-math.log(10000.0) / half_rot))
    angles = np.arange(length)[:, None] * freqs[None, :]
    cosine, sine = np.cos(angles), np.sin(angles)
    rest = np.zeros((length, HEAD - ROT))
    none = np.zeros_like(sine)
    tables = np.stack(
        [
            np.concatenate([cosine, cosine, rest + 1.0], axis=1),
            np.concatenate([-sine, none, rest], axis=1),
            np.concatenate([none, sine, rest], axis=1),
        ]
    )
    return jnp.asarray(np.tile(tables, (1, 1, heads)), F32)


MESH = pl.DeviceIdType.MESH
VMEM_BYTES = 60 * 2**20


def layer_kernel(
    lines,
    tok_ref,
    cot_ref,
    in_ref,
    out_ref,
    up_ref,
    down_ref,
    small_ref,
    table_ref,
    seq_ref,
    dy_ref,
    heads_ref,
    up_full_ref,
    down_full_ref,
    smalls_ref,
    normed_ref,
    act_ref,
    slope_ref,
    mixed_ref,
    proj_ref,
    pre_ref,
    grads_ref,
    land_ref,
    stage_ref,
    total_ref,
    final_ref,
    half_ref,
    twin_ref,
    pair_ref,
    owner_ref,
    proj_sum_ref,
    pre_sum_ref,
    small_v,
    small_f,
    gain_v,
    shift_v,
    in_bias_v,
    up_bias_v,
    local_sem,
    swap_send,
    swap_recv,
    team_send,
    team_recv,
    line_send,
    line_recv,
    sum_send,
    sum_recv,
    final_send,
    final_recv,
    twin_send,
    twin_recv,
    owner_send,
    owner_recv,
):
    dp = lax.axis_index("dp")
    mp = lax.axis_index("mp")
    quarter = dp % QUARTERS
    line = dp // QUARTERS
    other = 1 - mp
    core = dp % 2
    rows, width = tok_ref.shape
    depth = out_ref.shape[0]
    chunk = QUARTERS * depth
    wide = out_ref.shape[1] // QUARTERS
    unit = up_ref.shape[1] // QUARTERS
    tall = small_ref.shape[0]
    length = table_ref.shape[1]
    count = seq_ref.shape[0]
    has_above = line < lines - 1
    has_below = line > 0
    across, aside, twin = (dp ^ 2, mp), (dp, other), (dp ^ 1, mp)

    barrier = pltpu.get_barrier_semaphore()
    for peer in (twin, across, (dp ^ 3, mp), aside, (dp ^ 2, other)):
        pl.semaphore_signal(barrier, inc=1, device_id=peer, device_id_type=MESH)

    @pl.when(has_above)
    def _():
        pl.semaphore_signal(barrier, inc=1, device_id=(dp + QUARTERS, mp), device_id_type=MESH)

    @pl.when(has_below)
    def _():
        pl.semaphore_signal(barrier, inc=1, device_id=(dp - QUARTERS, mp), device_id_type=MESH)

    pl.semaphore_wait(barrier, 5 + has_above.astype(jnp.int32) + has_below.astype(jnp.int32))

    pending = []

    def begin(*copies):
        for copy in copies:
            copy.start()
            pending.append(copy)

    def remote(src, dst, send, recv, peer):
        return pltpu.make_async_remote_copy(
            src_ref=src,
            dst_ref=dst,
            send_sem=send,
            recv_sem=recv,
            device_id=peer,
            device_id_type=MESH,
        )

    def columns(index, size):
        return pl.ds(pl.multiple_of(index * size, size), size)

    def weight_views(device, to):
        mine, part = columns(device, depth), columns(device, depth)
        views = [
            (small_ref, smalls_ref.at[columns(device, tall), :]),
            (up_ref.at[:, columns(to, unit)], up_full_ref.at[mine, :]),
        ]
        for k in range(3):
            views.append(
                (in_ref.at[k, :, columns(to, wide)], heads_ref.at[part, pl.ds(k * wide, wide)])
            )
        views.append((out_ref.at[:, columns(to, wide)], heads_ref.at[part, pl.ds(3 * wide, wide)]))
        views.append((down_ref.at[:, columns(to, unit)], down_full_ref.at[part, :]))
        return views

    def swap(kind, j, device):
        src, dst = weight_views(device, quarter ^ j)[kind]
        return remote(
            src, dst, swap_send.at[kind, j - 1], swap_recv.at[kind, j - 1], (dp ^ j, mp)
        )

    own = [
        pltpu.make_async_copy(src, dst, local_sem.at[kind])
        for kind, (src, dst) in enumerate(weight_views(dp, quarter))
    ]

    def begin_swap(*kinds):
        for kind in kinds:
            begin(*[swap(kind, j, dp) for j in (2, 3, 1)])
            own[kind].start()

    def end_swap(*kinds):
        for kind in kinds:
            own[kind].wait()
            for j in (1, 2, 3):
                swap(kind, j, dp ^ j).wait_recv()

    def line_view(kind, index):
        if kind == 0:
            return smalls_ref.at[columns(index, QUARTERS * tall), :]
        return (up_full_ref, heads_ref, down_full_ref)[kind - 1].at[columns(index, chunk), :]

    def line_copy(kind, way, step, index):
        view = line_view(kind, index)
        return remote(
            view,
            view,
            line_send.at[kind, way, step - 1],
            line_recv.at[kind, way, step - 1],
            (dp + (QUARTERS if way == 0 else -QUARTERS), mp),
        )

    def sends(way, step):
        if way == 0:
            return (line >= step - 1) & has_above, line - (step - 1)
        return (line <= lines - step) & has_below, line + (step - 1)

    def takes(way, step):
        if way == 0:
            return line >= step, line - step
        return line <= lines - 1 - step, line + step

    def start_line(step, *kinds):
        if step < lines:
            for kind in kinds:
                for way in (0, 1):
                    go, index = sends(way, step)

                    @pl.when(go)
                    def _():
                        line_copy(kind, way, step, index).start()

    def wait_line(step, *kinds):
        if step < lines:
            for kind in kinds:
                for way in (0, 1):
                    go, index = takes(way, step)

                    @pl.when(go)
                    def _():
                        line_copy(kind, way, step, index).wait_recv()

    def line_step(step, *kinds):
        wait_line(step, *kinds)
        start_line(step + 1, *kinds)

    def line_rest(step, *kinds):
        for later in range(step, lines):
            line_step(later, *kinds)

    rows_of = ((tok_ref, seq_ref), (cot_ref, dy_ref))

    def seat(device, half_of):
        return columns((device % QUARTERS) * 2 + half_of, rows)

    def part_seat(device, half_of, part):
        low = rows // 4 * 3
        start = ((device % QUARTERS) * 2 + half_of) * rows + part * low
        size = rows - low if part else low
        return pl.ds(pl.multiple_of(start, rows // 4), size)

    def relay(which, number, place, peer):
        view = rows_of[which][1].at[place, :]
        return remote(view, view, team_send.at[which, number], team_recv.at[which, number], peer)

    def offer(which, number, peer):
        src, dst = rows_of[which]
        return remote(
            src,
            dst.at[seat(dp, mp), :],
            team_send.at[which, number],
            team_recv.at[which, number],
            peer,
        )

    own_rows = [
        pltpu.make_async_copy(src, dst.at[seat(dp, mp), :], local_sem.at[7 + which])
        for which, (src, dst) in enumerate(rows_of)
    ]
    near, beside = seat(dp ^ 2, mp), seat(dp, other)

    def pass_on(which):
        relay(which, 0, near, across).wait_recv()
        begin(
            relay(which, 3, part_seat(dp ^ 2, mp, 0), aside),
            relay(which, 4, near, twin),
        )
        relay(which, 1, beside, aside).wait_recv()
        begin(
            relay(which, 5, part_seat(dp, other, 1), across),
            relay(which, 6, beside, twin),
        )

    def hand_over(which):
        for part, peer in ((0, aside), (1, across)):
            far = part_seat(dp ^ 2, other, part)
            relay(which, 3 + 2 * part, far, peer).wait_recv()
            begin(relay(which, 7 + part, far, twin))

    def all_rows(which):
        own_rows[which].wait()
        relay(which, 2, seat(dp ^ 1, mp), twin).wait_recv()
        relay(which, 4, seat(dp ^ 3, mp), twin).wait_recv()
        relay(which, 6, seat(dp ^ 1, other), twin).wait_recv()
        for part in (0, 1):
            relay(which, 7 + part, part_seat(dp ^ 3, other, part), twin).wait_recv()

    def dot(a, b, contract):
        return lax.dot_general(a, b, (contract, ((), ())), preferred_element_type=F32)

    nn, nt, tn = ((1,), (0,)), ((1,), (1,)), ((0,), (0,))
    tile = min(256, count)

    def pipeline(body, grid, in_specs, out_specs, *refs):
        pltpu.emit_pipeline(
            body, grid=grid, in_specs=in_specs, out_specs=out_specs, _explicit_indices=True
        )(*refs)

    def row_blocks(size, columns_, place=0):
        return pl.BlockSpec((size, columns_), lambda i: (i, place))

    def fixed(shape, *place):
        return pl.BlockSpec(shape, lambda i: place or (0,) * len(shape))

    def normalize_rows():
        def body(step, rows_in, rows_out):
            unit_rows = normalize(rows_in[...].astype(F32))[0]
            rows_out[...] = (unit_rows * gain_v[...] + shift_v[...]).astype(BF16)

        pipeline(
            body,
            (count // tile,),
            [row_blocks(tile, width)],
            [row_blocks(tile, width)],
            seq_ref,
            normed_ref,
        )

    def activate():
        def body(step, rows_in, weight, act, slope):
            u = dot(rows_in[...], weight[...], nn) + up_bias_v[...]
            value, derivative = smooth_gate(u)
            act[...] = value.astype(BF16)
            slope[...] = derivative.astype(BF16)

        pipeline(
            body,
            (count // tile,),
            [row_blocks(tile, width), fixed((width, unit))],
            [row_blocks(tile, unit), row_blocks(tile, unit)],
            normed_ref,
            up_full_ref,
            act_ref,
            slope_ref,
        )

    tall_tile = min(512, width)

    def weight_grad(left, right, right_wide, kind, start=0):
        def body(step, a, b, out):
            out[...] = dot(a[...], b[...], tn).astype(BF16)

        pipeline(
            body,
            (width // tall_tile,),
            [
                pl.BlockSpec((count, tall_tile), lambda i: (0, i)),
                fixed((count, right_wide)),
            ],
            [row_blocks(tall_tile, right_wide)],
            left,
            right,
            grads_ref.at[kind, :, pl.ds(start, right_wide)],
        )

    def attend(first, last):
        def shifted(columns_):
            return pl.BlockSpec((length, columns_), lambda i: (i + first, 0))

        def body(step, rows_in, dys, weight, mixed, proj):
            pre = dot(rows_in[...], weight[:, : 3 * wide], nn) + in_bias_v[...]
            douts = dot(dys[...], weight[:, 3 * wide :], nn).astype(BF16)
            value, backs = attention_block(
                [pre[:, k * wide : (k + 1) * wide] for k in range(3)],
                [table_ref[k] for k in range(3)],
                douts,
            )
            mixed[...] = value
            for k in range(3):
                proj[:, k * wide : (k + 1) * wide] = backs[k]
                part = jnp.sum(backs[k].astype(F32), axis=0, keepdims=True)
                place = slice(k * wide, (k + 1) * wide)

                proj_sum_ref[:, place] = proj_sum_ref[:, place] + part

        pipeline(
            body,
            (last - first,),
            [shifted(width), shifted(width), fixed((width, 4 * wide))],
            [shifted(wide), shifted(3 * wide)],
            normed_ref,
            dy_ref,
            heads_ref,
            mixed_ref,
            proj_ref,
        )

    def gate_back():
        def body(step, dys, weight, slope, pre):
            value = (dot(dys[...], weight[...], nn) * slope[...].astype(F32)).astype(BF16)
            pre[...] = value
            part = jnp.sum(value.astype(F32), axis=0, keepdims=True)

            @pl.when(step.index[0] == 0)
            def _():
                pre_sum_ref[...] = part

            @pl.when(step.index[0] > 0)
            def _():
                pre_sum_ref[...] = pre_sum_ref[...] + part

        pipeline(
            body,
            (count // tile,),
            [row_blocks(tile, width), fixed((width, unit)), row_blocks(tile, unit)],
            [row_blocks(tile, unit)],
            dy_ref,
            down_full_ref,
            slope_ref,
            pre_ref,
        )

    def back_to_rows(which, wide_rows, wide_weight, thin_rows, thin_wide, start, half_of, got):
        per = length // tile
        grid = (QUARTERS // 2 * per,)

        def rows_at(i):
            return ((i // per) * 2 + half_of) * per + i % per

        def body(step, a, weight, b, thin, *rest):
            sums = dot(a[...], weight[...], nt) + dot(b[...], thin[...], nt)
            if got:
                sums = sums + rest[0][...].astype(F32)
            rest[-1][...] = sums.astype(BF16)

        in_specs = [
            pl.BlockSpec((tile, unit), lambda i: (rows_at(i), 0)),
            fixed((width, unit)),
            pl.BlockSpec((tile, thin_wide), lambda i: (rows_at(i), 0)),
            fixed((width, thin_wide)),
        ]
        refs = [wide_rows, wide_weight, thin_rows, heads_ref.at[:, pl.ds(start, thin_wide)]]
        if got:
            in_specs.append(row_blocks(tile, width))
            refs.append(twin_ref.at[which])
        refs.append(pair_ref.at[which] if got else half_ref.at[which])
        pipeline(body, grid, in_specs, [row_blocks(tile, width)], *refs)

    def forward_rows(half_of, got):
        back_to_rows(0, act_ref, down_full_ref, mixed_ref, wide, 3 * wide, half_of, got)

    def backward_rows(half_of, got):
        back_to_rows(1, pre_ref, up_full_ref, proj_ref, 3 * wide, 0, half_of, got)

    def twin_copy(which):
        return remote(
            half_ref.at[which], twin_ref.at[which], twin_send.at[which], twin_recv.at[which], twin
        )

    def owner_copy(which, number, peer, place):
        return remote(
            pair_ref.at[which, columns(place, rows), :],
            owner_ref.at[which, number],
            owner_send.at[which, number],
            owner_recv.at[which, number],
            peer,
        )

    chip = (dp // 2) % (QUARTERS // 2)

    def to_owners(which):
        begin(
            owner_copy(which, 2, (dp ^ 2, other), (1 - chip) * 2 + other),
            owner_copy(which, 0, across, (1 - chip) * 2 + mp),
            owner_copy(which, 1, aside, chip * 2 + other),
        )

    add_tile = min(256, chunk)

    def add_chunks(dst, *parts):
        def body(step, *refs):
            *ins, out = refs
            out[...] = sum(ref[...].astype(F32) for ref in ins).astype(BF16)

        pipeline(
            body,
            (chunk // add_tile,),
            [row_blocks(add_tile, unit)] * len(parts),
            [row_blocks(add_tile, unit)],
            *parts,
            dst,
        )

    def sum_sends(way, step):
        far = lines - step
        if way == 0:
            return (line <= step - 1) & has_above, line + far, line == 0
        return (line >= lines - step) & has_below, line - far, line == lines - 1

    def sum_takes(way, step):
        if way == 0:
            return has_below & (line <= step)
        return has_above & (line >= lines - 1 - step)

    def sum_copy(kind, way, step, src):
        return remote(
            src,
            land_ref.at[kind, way, step - 1],
            sum_send.at[kind, way, step - 1],
            sum_recv.at[kind, way, step - 1],
            (dp + (QUARTERS if way == 0 else -QUARTERS), mp),
        )

    def sum_start(kind, step):
        if step < lines:
            for way in (0, 1):
                go, index, first = sum_sends(way, step)
                view = grads_ref.at[kind, columns(index, chunk), :]

                @pl.when(go & first)
                def _():
                    sum_copy(kind, way, step, view).start()

                if step > 1:

                    @pl.when(go & ~first)
                    def _():
                        staged = stage_ref.at[kind, way, step - 1]
                        add_chunks(staged, view, land_ref.at[kind, way, step - 2])
                        sum_copy(kind, way, step, staged).start()

    def sum_wait(kind, step):
        if step < lines:
            for way in (0, 1):

                @pl.when(sum_takes(way, step))
                def _():
                    sum_copy(kind, way, step, stage_ref.at[kind, way, step - 1]).wait_recv()

    def sum_step(kind, step):
        sum_wait(kind, step)
        sum_start(kind, step + 1)

    def final_copy(kind, j):
        return remote(
            total_ref.at[kind, columns(quarter ^ j, depth), :],
            final_ref.at[kind, quarter],
            final_send.at[kind, j - 1],
            final_recv.at[kind, j - 1],
            (dp ^ j, mp),
        )

    def final_in(kind, j):
        return remote(
            total_ref.at[kind, columns(quarter, depth), :],
            final_ref.at[kind, quarter ^ j],
            final_send.at[kind, j - 1],
            final_recv.at[kind, j - 1],
            (dp ^ j, mp),
        )

    def final_own(kind):
        return pltpu.make_async_copy(
            total_ref.at[kind, columns(quarter, depth), :],
            final_ref.at[kind, quarter],
            local_sem.at[10 + kind],
        )

    def sum_total(kind, step):
        for later in range(step, lines):
            sum_step(kind, later)
        view = grads_ref.at[kind, columns(line, chunk), :]
        below = land_ref.at[kind, 0, lines - 2]
        above = land_ref.at[kind, 1, lines - 2]

        @pl.when(has_below & has_above)
        def _():
            add_chunks(total_ref.at[kind], view, below, above)

        @pl.when(has_below & ~has_above)
        def _():
            add_chunks(total_ref.at[kind], view, below)

        @pl.when(has_above & ~has_below)
        def _():
            add_chunks(total_ref.at[kind], view, above)

        begin(*[final_copy(kind, j) for j in (2, 3, 1)])
        final_own(kind).start()

    begin_swap(0, 1)
    begin(offer(0, 1, aside), offer(0, 2, twin))
    own_rows[0].start()
    own_rows[1].start()
    end_swap(0, 1)
    start_line(1, 0, 1)
    begin(offer(0, 0, across), offer(1, 1, aside), offer(1, 2, twin))
    line_step(1, 0, 1)
    pass_on(0)
    begin_swap(2, 3, 4, 5)
    begin(offer(1, 0, across))
    hand_over(0)
    line_step(2, 0, 1)
    end_swap(2, 3, 4, 5)
    start_line(1, 2)
    all_rows(0)
    line_rest(3, 0)
    fetch = pltpu.make_async_copy(smalls_ref, small_v, local_sem.at[9])
    fetch.start()
    fetch.wait()
    small_f[...] = small_v[...].astype(F32)
    each = width // (lines * QUARTERS)
    for d in range(lines * QUARTERS):
        place = slice(d * each, (d + 1) * each)
        gain_v[:, place] = small_f[d * tall : d * tall + 1, :each]
        shift_v[:, place] = small_f[d * tall + 1 : d * tall + 2, :each]
    in_each = wide // lines
    up_each = unit // lines
    up_low = min(up_each, 128)
    for i in range(lines):
        top = pl.multiple_of((quarter * lines + i) * tall, tall)
        block = small_f[pl.ds(top, tall), :]
        for k in range(3):
            start = k * wide + i * in_each
            in_bias_v[:, start : start + in_each] = block[4 + k : 5 + k, :in_each]
        for r in range(up_each // up_low):
            start = i * up_each + r * up_low
            up_bias_v[:, start : start + up_low] = block[7 + r : 8 + r, :up_low]
    normalize_rows()
    pass_on(1)
    line_rest(3, 1)
    activate()
    hand_over(1)
    begin_swap(6)
    line_step(1, 2)
    all_rows(1)
    weight_grad(dy_ref, act_ref, unit, 0)
    sum_start(0, 1)
    line_step(2, 2)
    end_swap(6)
    sum_step(0, 1)
    line_rest(3, 2)
    start_line(1, 3)

    groups = count // length
    proj_sum_ref[...] = jnp.zeros_like(proj_sum_ref)
    attend(0, groups // 2)
    sum_step(0, 2)
    attend(groups // 2, groups)
    line_step(1, 3)
    weight_grad(dy_ref, mixed_ref, wide, 1, 3 * wide)
    line_step(2, 3)
    weight_grad(normed_ref, proj_ref, 3 * wide, 1, 0)
    sum_start(1, 1)
    sum_total(0, 3)
    sum_step(1, 1)
    line_rest(3, 3)
    gate_back()
    sum_step(1, 2)
    weight_grad(normed_ref, pre_ref, unit, 2)
    sum_start(2, 1)
    forward_rows(1 - core, False)
    begin(twin_copy(0))
    sum_step(2, 1)
    backward_rows(1 - core, False)
    begin(twin_copy(1))
    sum_total(1, 3)
    twin_copy(0).wait_recv()
    forward_rows(core, True)
    to_owners(0)
    sum_step(2, 2)
    twin_copy(1).wait_recv()
    backward_rows(core, True)
    to_owners(1)
    sum_total(2, 3)

    for which in (0, 1):
        for number, peer in ((0, across), (1, aside), (2, (dp ^ 2, other))):
            owner_copy(which, number, peer, 0).wait_recv()
    for kind in range(3):
        final_own(kind).wait()
        for j in (1, 2, 3):
            final_in(kind, j).wait_recv()
    for copy in pending:
        copy.wait_send()
    for step in range(1, lines):
        for way in (0, 1):
            go, index = sends(way, step)
            sent, which, first = sum_sends(way, step)

            @pl.when(go)
            def _():
                for kind in range(4):
                    line_copy(kind, way, step, index).wait_send()

            @pl.when(sent)
            def _():
                for kind in range(3):
                    sum_copy(kind, way, step, stage_ref.at[kind, way, step - 1]).wait_send()


def run_layer(lines, team, tokens, cotangent, in_weight, out_weight, up_weight, down_weight, small, table):
    rows, width = tokens.shape
    depth = out_weight.shape[0]
    wide = out_weight.shape[1] // QUARTERS
    unit = up_weight.shape[1] // QUARTERS
    chunk = QUARTERS * depth
    whole = lines * chunk
    count = team * rows
    smalls = lines * QUARTERS * small.shape[0]
    steps = max(lines - 1, 1)
    anywhere = pl.BlockSpec(memory_space=pl.ANY)
    inside = pl.BlockSpec(memory_space=pltpu.VMEM)

    def low(*shape):
        return jax.ShapeDtypeStruct(shape, BF16)

    outs = [
        low(count, width),
        low(count, width),
        low(whole, 4 * wide),
        low(whole, unit),
        low(whole, unit),
        low(smalls, 128),
        low(count, width),
        low(count, unit),
        low(count, unit),
        low(count, wide),
        low(count, 3 * wide),
        low(count, unit),
        low(3, width, unit),
        low(3, 2, steps, chunk, unit),
        low(3, 2, steps, chunk, unit),
        low(3, chunk, unit),
        low(3, QUARTERS, depth, unit),
        low(2, count // 2, width),
        low(2, count // 2, width),
        low(2, count // 2, width),
        low(2, 3, rows, width),
    ]
    sums = [
        jax.ShapeDtypeStruct((1, 3 * wide), F32),
        jax.ShapeDtypeStruct((1, unit), F32),
    ]
    dma = pltpu.SemaphoreType.DMA
    results = pl.pallas_call(
        functools.partial(layer_kernel, lines),
        out_shape=outs + sums,
        in_specs=[anywhere] * 7 + [inside],
        out_specs=[anywhere] * len(outs) + [inside] * 2,
        scratch_shapes=[
            pltpu.VMEM((smalls, 128), BF16),
            pltpu.VMEM((smalls, 128), F32),
            pltpu.VMEM((1, width), F32),
            pltpu.VMEM((1, width), F32),
            pltpu.VMEM((1, 3 * wide), F32),
            pltpu.VMEM((1, unit), F32),
            dma((13,)),
            dma((7, 3)),
            dma((7, 3)),
            dma((2, 9)),
            dma((2, 9)),
            dma((4, 2, steps)),
            dma((4, 2, steps)),
            dma((3, 2, steps)),
            dma((3, 2, steps)),
            dma((3, 3)),
            dma((3, 3)),
            dma((2,)),
            dma((2,)),
            dma((2, 3)),
            dma((2, 3)),
        ],
        compiler_params=pltpu.CompilerParams(
            collective_id=1, has_side_effects=True, vmem_limit_bytes=VMEM_BYTES
        ),
    )(tokens, cotangent, in_weight, out_weight, up_weight, down_weight, small, table)
    return results[5], results[16], results[19], results[20], results[21], results[22]


def small_kernel(lines, both, vec_ref, total_ref, land_a, part, land_b, land_c, send, recv):
    dp = lax.axis_index("dp")
    mp = lax.axis_index("mp")
    quarter = dp % QUARTERS
    line = dp // QUARTERS
    aside = (dp, 1 - mp)

    def in_line(k):
        return (lax.rem(line + k, lines) * QUARTERS + quarter, mp)

    barrier = pltpu.get_barrier_semaphore()
    peers = [(dp ^ j, mp) for j in (1, 2, 3)] + [in_line(k) for k in range(1, lines)] + [aside]
    for peer in peers:
        pl.semaphore_signal(barrier, inc=1, device_id=peer, device_id_type=MESH)
    pl.semaphore_wait(barrier, len(peers))

    def move(number, src, dst, peer):
        return pltpu.make_async_remote_copy(
            src_ref=src,
            dst_ref=dst,
            send_sem=send.at[number],
            recv_sem=recv.at[number],
            device_id=peer,
            device_id_type=MESH,
        )

    first = [
        move(j - 1, vec_ref.at[quarter ^ j], land_a.at[j - 1], (dp ^ j, mp)) for j in (1, 2, 3)
    ]
    for copy in first:
        copy.start()
    for copy in first:
        copy.wait()
    part[...] = (vec_ref[quarter] + land_a[0]) + (land_a[1] + land_a[2])
    second = [
        move(2 + k, part.at[lax.rem(line + k, lines)], land_b.at[k - 1], in_line(k))
        for k in range(1, lines)
    ]
    for copy in second:
        copy.start()
    total = part[line]
    for k, copy in enumerate(second):
        copy.wait()
        total = total + land_b[k]
    total_ref[...] = total
    third = move(2 + lines, total_ref, land_c, aside)
    third.start()
    third.wait()
    shape = total_ref.shape
    index = lax.broadcasted_iota(jnp.int32, shape, 0) * shape[1]
    index = index + lax.broadcasted_iota(jnp.int32, shape, 1)
    total_ref[...] = jnp.where(index < both, total + land_c[...], total)


def sum_small(lines, both, vector):
    tile = vector.shape[2:]
    count = lines + 3
    return pl.pallas_call(
        functools.partial(small_kernel, lines, both),
        out_shape=jax.ShapeDtypeStruct(tile, F32),
        in_specs=[pl.BlockSpec(memory_space=pltpu.VMEM)],
        out_specs=pl.BlockSpec(memory_space=pltpu.VMEM),
        scratch_shapes=[
            pltpu.VMEM((3, lines) + tile, F32),
            pltpu.VMEM((lines,) + tile, F32),
            pltpu.VMEM((max(lines - 1, 1),) + tile, F32),
            pltpu.VMEM(tile, F32),
            pltpu.SemaphoreType.DMA((count,)),
            pltpu.SemaphoreType.DMA((count,)),
        ],
        compiler_params=pltpu.CompilerParams(collective_id=2, has_side_effects=True),
    )(vector)


def smooth_gate(u):
    slope = math.sqrt(2.0 / math.pi)
    square = u * u
    curve = jnp.tanh(slope * (u + 0.044715 * (u * square)))
    rise = 0.5 * (1.0 + curve)
    bend = 0.5 * u * (1.0 - curve * curve) * (slope * (1.0 + 3.0 * 0.044715 * square))
    return u * rise, rise + bend


def per_device(
    tokens,
    norm_gain,
    norm_shift,
    in_weight,
    in_bias,
    out_weight,
    out_bias,
    up_weight,
    up_bias,
    down_weight,
    down_bias,
    cotangent,
):
    n_dp = lax.axis_size("dp")
    n_mp = lax.axis_size("mp")
    lines = n_dp // QUARTERS
    dp = lax.axis_index("dp")
    mp = lax.axis_index("mp")
    quarter = dp % QUARTERS
    chip = (dp // 2) % (QUARTERS // 2)
    own_rows, width = tokens.shape
    rows_here = in_weight.shape[1]
    each = norm_gain.shape[0]
    in_each = in_bias.shape[1]
    up_each = up_bias.shape[0]
    wide = out_weight.shape[1] // QUARTERS

    def row(vector):
        return jnp.pad(vector, (0, -vector.shape[0] % 128)).reshape(-1, 128)

    small = jnp.concatenate(
        [row(norm_gain), row(norm_shift), row(out_bias), row(down_bias)]
        + [row(in_bias[k]) for k in range(3)]
        + [row(up_bias)]
    )
    small = jnp.pad(small, ((0, SMALL - small.shape[0]), (0, 0)))
    table = rotary_tables(n_mp * own_rows, wide // HEAD)
    smalls, final, pair, owner, grad_in_bias, grad_up_bias = run_layer(
        lines, QUARTERS * n_mp, tokens, cotangent, in_weight, out_weight, up_weight, down_weight, small, table
    )
    smalls = smalls.reshape(n_dp, SMALL, 128)[:, :, :each].astype(F32)
    full_gain = smalls[:, 0].reshape(-1)
    full_out_bias = smalls[:, 2].reshape(-1)
    full_down_bias = smalls[:, 3].reshape(-1)

    def place(buffer, piece, index, axis):
        return lax.dynamic_update_index_in_dim(buffer, piece, index, axis)

    mine = lax.dynamic_slice_in_dim(pair, (chip * 2 + mp) * own_rows, own_rows, 1).astype(F32)
    sums = mine + owner[:, 0].astype(F32) + owner[:, 1].astype(F32) + owner[:, 2].astype(F32)
    summed, grad_own = sums[0], sums[1]
    outcome = (tokens.astype(F32) + summed + full_out_bias + full_down_bias).astype(BF16)
    final = final.astype(F32).transpose(0, 2, 1, 3)
    own_grad_down = final[0]
    own_grad_up = final[2]
    own_heads = final[1].reshape(rows_here, QUARTERS, 4, wide).transpose(2, 0, 1, 3)
    own_grad_in, own_grad_out = own_heads[:3], own_heads[3]
    own_unit, own_inv = normalize(tokens.astype(F32))
    gain_part = jnp.sum(grad_own * own_unit, axis=0)
    shift_part = jnp.sum(grad_own, axis=0)
    bias_part = jnp.sum(cotangent.astype(F32), axis=0)
    scaled = grad_own * full_gain
    centered_grad = (
        scaled
        - jnp.mean(scaled, axis=-1, keepdims=True)
        - own_unit * jnp.mean(scaled * own_unit, axis=-1, keepdims=True)
    )
    grad_input = cotangent.astype(F32) + own_inv * centered_grad

    wide = jnp.stack([gain_part, shift_part, bias_part])
    wide = wide.reshape(3, lines, QUARTERS, each).transpose(2, 1, 0, 3)
    wide = wide.reshape(QUARTERS, lines, 3 * each)
    in_blocks = grad_in_bias.reshape(3, lines, in_each).transpose(1, 0, 2).reshape(lines, -1)
    mine = jnp.concatenate([in_blocks, grad_up_bias.reshape(lines, up_each)], axis=1)
    spread = place(jnp.zeros((QUARTERS,) + mine.shape, F32), mine, quarter, 0)
    spread = spread.reshape(lines, QUARTERS, -1).transpose(1, 0, 2)
    vector = jnp.concatenate([wide, spread], axis=2)
    vector = jnp.pad(vector, ((0, 0), (0, 0), (0, 1024 - vector.shape[2])))
    owned = sum_small(lines, 3 * each, vector.reshape(QUARTERS, lines, 8, 128)).reshape(-1)
    own_gain = owned[:each]
    own_shift = owned[each : 2 * each]
    own_bias = owned[2 * each : 3 * each]
    own_in_bias = owned[3 * each : 3 * each + 3 * in_each].reshape(3, in_each)
    own_up_bias = owned[3 * each + 3 * in_each : 3 * each + 3 * in_each + up_each]

    return (
        outcome,
        grad_input,
        own_gain,
        own_shift,
        own_grad_in.reshape(in_weight.shape),
        own_in_bias,
        own_grad_out.reshape(out_weight.shape),
        own_bias,
        own_grad_up.reshape(up_weight.shape),
        own_up_bias,
        own_grad_down.reshape(down_weight.shape),
        own_bias,
    )


def solution(mesh):
    return jax.shard_map(
        per_device,
        mesh=mesh,
        in_specs=(
            P(("dp", "mp"), None),
            P("dp"),
            P("dp"),
            P(None, "dp", "mp"),
            P(None, ("mp", "dp")),
            P("dp", "mp"),
            P("dp"),
            P("dp", "mp"),
            P(("mp", "dp")),
            P("dp", "mp"),
            P("dp"),
            P(("dp", "mp"), None),
        ),
        out_specs=(
            P(("dp", "mp"), None),
            P(("dp", "mp"), None),
            P("dp"),
            P("dp"),
            P(None, "dp", "mp"),
            P(None, ("mp", "dp")),
            P("dp", "mp"),
            P("dp"),
            P("dp", "mp"),
            P(("mp", "dp")),
            P("dp", "mp"),
            P("dp"),
        ),
        check_vma=False,
    )
```

```python
import functools
import math

import jax
import jax.numpy as jnp
import numpy as np
from jax import lax
from jax.experimental import pallas as pl
from jax.experimental.pallas import tpu as pltpu
from jax.sharding import PartitionSpec as P

HEAD = 64
ROT = 32
QUARTERS = 4
SMALL = 16
norm_eps = 1e-05
F32 = jnp.float32
BF16 = jnp.bfloat16


def normalize(rows):
    middle = jnp.mean(rows, axis=-1, keepdims=True)
    centered = rows - middle
    spread = jnp.mean(centered * centered, axis=-1, keepdims=True)
    inv_spread = lax.rsqrt(spread + norm_eps)
    return (centered * inv_spread, inv_spread)


def roll_lanes(v, by):
    return pltpu.roll(v, by, 1)


def attention_block(pre, table, douts):
    length, wide = douts.shape
    heads = wide // HEAD
    block = length // 2
    half_rot = ROT // 2
    scale = 1.0 / math.sqrt(HEAD)
    cosine, first, second = table

    def turn(v):
        return (
            v * cosine
            + roll_lanes(v, wide - half_rot) * first
            + roll_lanes(v, half_rot) * second
        )

    def turn_back(g):
        return (
            g * cosine
            + roll_lanes(g * first, half_rot)
            + roll_lanes(g * second, wide - half_rot)
        )

    queries = turn(pre[0]).astype(BF16)
    keys = turn(pre[1]).astype(BF16)
    values = pre[2].astype(BF16)
    head_of = lax.broadcasted_iota(jnp.int32, (block, wide), 1) // HEAD
    nothing = jnp.zeros((block, wide), BF16)
    mixed = [None, None]
    dq, dk, dv = [None, None], [None, None], [None, None]

    def dot(a, b, contract):
        return lax.dot_general(a, b, (contract, ((), ())), preferred_element_type=F32)

    def add(total, part):
        return part if total is None else total + part

    for head in range(heads):
        here = head_of == head

        def only(v):
            return jnp.where(here, v, nothing)

        q_here = [only(queries[i * block : (i + 1) * block]) for i in range(2)]
        k_here = [only(keys[i * block : (i + 1) * block]) for i in range(2)]
        v_here = [only(values[i * block : (i + 1) * block]) for i in range(2)]
        d_here = [only(douts[i * block : (i + 1) * block]) for i in range(2)]
        for i in range(2):
            seen = (i + 1) * block
            scores = dot(q_here[i], keys[:seen], ((1,), (1,))) * scale
            row = lax.broadcasted_iota(jnp.int32, (block, seen), 0) + i * block
            col = lax.broadcasted_iota(jnp.int32, (block, seen), 1)
            scores = jnp.where(col <= row, scores, -1e30)
            powers = jnp.exp(scores - jnp.max(scores, axis=1, keepdims=True))
            probs = powers * (1.0 / jnp.sum(powers, axis=1, keepdims=True))
            low = probs.astype(BF16)
            dprobs = dot(d_here[i], values[:seen], ((1,), (1,)))
            total = jnp.sum(probs * dprobs, axis=1, keepdims=True)
            dscores = (probs * (dprobs - total)).astype(BF16)
            for j in range(i + 1):
                part = slice(j * block, (j + 1) * block)
                mixed[i] = add(mixed[i], dot(low[:, part], v_here[j], ((1,), (0,))))
                dq[i] = add(dq[i], dot(dscores[:, part], k_here[j], ((1,), (0,))))
                dv[j] = add(dv[j], dot(low[:, part], d_here[i], ((0,), (0,))))
                dk[j] = add(dk[j], dot(dscores[:, part], q_here[i], ((0,), (0,))))
    value = jnp.concatenate(mixed, axis=0).astype(BF16)
    dq_low = (jnp.concatenate(dq, axis=0) * scale).astype(BF16)
    dk_low = (jnp.concatenate(dk, axis=0) * scale).astype(BF16)
    backs = (
        turn_back(dq_low.astype(F32)).astype(BF16),
        turn_back(dk_low.astype(F32)).astype(BF16),
        jnp.concatenate(dv, axis=0).astype(BF16),
    )
    return value, backs


def rotary_tables(length, heads):
    half_rot = ROT // 2
    freqs = np.exp(np.arange(half_rot) * (-math.log(10000.0) / half_rot))
    angles = np.arange(length)[:, None] * freqs[None, :]
    cosine, sine = np.cos(angles), np.sin(angles)
    rest = np.zeros((length, HEAD - ROT))
    none = np.zeros_like(sine)
    tables = np.stack(
        [
            np.concatenate([cosine, cosine, rest + 1.0], axis=1),
            np.concatenate([-sine, none, rest], axis=1),
            np.concatenate([none, sine, rest], axis=1),
        ]
    )
    return jnp.asarray(np.tile(tables, (1, 1, heads)), F32)


MESH = pl.DeviceIdType.MESH
VMEM_BYTES = 60 * 2**20


def layer_kernel(
    lines,
    tok_ref,
    cot_ref,
    in_ref,
    out_ref,
    up_ref,
    down_ref,
    small_ref,
    table_ref,
    seq_ref,
    dy_ref,
    heads_ref,
    up_full_ref,
    down_full_ref,
    smalls_ref,
    normed_ref,
    act_ref,
    slope_ref,
    mixed_ref,
    proj_ref,
    pre_ref,
    grads_ref,
    land_ref,
    stage_ref,
    total_ref,
    half_ref,
    twin_ref,
    pair_ref,
    owner_ref,
    result_ref,
    grad_ref,
    final_down_ref,
    final_up_ref,
    final_in_ref,
    final_out_ref,
    own_small_ref,
    proj_sum_ref,
    pre_sum_ref,
    gain_sum,
    shift_sum,
    dy_sum,
    vector,
    vector_land,
    part,
    part_land,
    aside_land,
    small_v,
    small_f,
    gain_v,
    shift_v,
    out_bias_v,
    in_bias_v,
    up_bias_v,
    local_sem,
    swap_send,
    swap_recv,
    team_send,
    team_recv,
    line_send,
    line_recv,
    sum_send,
    sum_recv,
    final_send,
    final_recv,
    twin_send,
    twin_recv,
    owner_send,
    owner_recv,
    small_send,
    small_recv,
):
    dp = lax.axis_index("dp")
    mp = lax.axis_index("mp")
    quarter = dp % QUARTERS
    line = dp // QUARTERS
    other = 1 - mp
    core = dp % 2
    rows, width = tok_ref.shape
    depth = out_ref.shape[0]
    chunk = QUARTERS * depth
    wide = out_ref.shape[1] // QUARTERS
    unit = up_ref.shape[1] // QUARTERS
    tall = small_ref.shape[0]
    length = table_ref.shape[1]
    count = seq_ref.shape[0]
    each = width // (lines * QUARTERS)
    in_each = wide // lines
    up_each = unit // lines
    up_low = min(up_each, 128)
    has_above = line < lines - 1
    has_below = line > 0
    across, aside, twin = (dp ^ 2, mp), (dp, other), (dp ^ 1, mp)

    barrier = pltpu.get_barrier_semaphore()
    def in_line(k):
        return (lax.rem(line + k, lines) * QUARTERS + quarter, mp)

    peers = [twin, across, (dp ^ 3, mp), aside, (dp ^ 2, other)]
    peers += [in_line(k) for k in range(1, lines)]
    for peer in peers:
        pl.semaphore_signal(barrier, inc=1, device_id=peer, device_id_type=MESH)
    pl.semaphore_wait(barrier, len(peers))

    pending = []
    expected = {}

    def begin(*copies):
        for copy in copies:
            copy.start()
            pending.append(copy.wait_send)

    def arrive(*key):
        expected.pop(key)()

    def remote(src, dst, send, recv, peer):
        return pltpu.make_async_remote_copy(
            src_ref=src,
            dst_ref=dst,
            send_sem=send,
            recv_sem=recv,
            device_id=peer,
            device_id_type=MESH,
        )

    def columns(index, size):
        return pl.ds(pl.multiple_of(index * size, size), size)

    def weight_views(device, to):
        mine, part = columns(device, depth), columns(device, depth)
        views = [
            (small_ref, smalls_ref.at[columns(device, tall), :]),
            (up_ref.at[:, columns(to, unit)], up_full_ref.at[mine, :]),
        ]
        for k in range(3):
            views.append(
                (in_ref.at[k, :, columns(to, wide)], heads_ref.at[part, pl.ds(k * wide, wide)])
            )
        views.append((out_ref.at[:, columns(to, wide)], heads_ref.at[part, pl.ds(3 * wide, wide)]))
        views.append((down_ref.at[:, columns(to, unit)], down_full_ref.at[part, :]))
        return views

    def swap(kind, j, device):
        src, dst = weight_views(device, quarter ^ j)[kind]
        return remote(
            src, dst, swap_send.at[kind, j - 1], swap_recv.at[kind, j - 1], (dp ^ j, mp)
        )

    own = [
        pltpu.make_async_copy(src, dst, local_sem.at[kind])
        for kind, (src, dst) in enumerate(weight_views(dp, quarter))
    ]

    def begin_swap(*kinds):
        for kind in kinds:
            begin(*[swap(kind, j, dp) for j in (2, 3, 1)])
            own[kind].start()

            def wait(kind=kind):
                own[kind].wait()
                for j in (1, 2, 3):
                    swap(kind, j, dp ^ j).wait_recv()

            expected["swap", kind] = wait

    def end_swap(*kinds):
        for kind in kinds:
            arrive("swap", kind)

    def line_view(kind, index):
        if kind == 0:
            return smalls_ref.at[columns(index, QUARTERS * tall), :]
        return (up_full_ref, heads_ref, down_full_ref)[kind - 1].at[columns(index, chunk), :]

    def line_copy(kind, way, step, index):
        view = line_view(kind, index)
        return remote(
            view,
            view,
            line_send.at[kind, way, step - 1],
            line_recv.at[kind, way, step - 1],
            (dp + (QUARTERS if way == 0 else -QUARTERS), mp),
        )

    def sends(way, step):
        if way == 0:
            return (line >= step - 1) & has_above, line - (step - 1)
        return (line <= lines - step) & has_below, line + (step - 1)

    def takes(way, step):
        if way == 0:
            return line >= step, line - step
        return line <= lines - 1 - step, line + step

    def when(go, act):
        @pl.when(go)
        def _():
            act()

    def start_line(step, *kinds):
        if step < lines:
            for kind in kinds:
                for way in (0, 1):
                    go, index = sends(way, step)
                    copy = line_copy(kind, way, step, index)
                    when(go, copy.start)

                def left(kind=kind):
                    for way in (0, 1):
                        go, index = sends(way, step)
                        when(go, line_copy(kind, way, step, index).wait_send)

                pending.append(left)

                def wait(kind=kind):
                    for way in (0, 1):
                        go, index = takes(way, step)
                        when(go, line_copy(kind, way, step, index).wait_recv)

                expected["line", kind, step] = wait

    def wait_line(step, *kinds):
        if step < lines:
            for kind in kinds:
                arrive("line", kind, step)

    def line_step(step, *kinds):
        wait_line(step, *kinds)
        start_line(step + 1, *kinds)

    def line_rest(step, *kinds):
        for later in range(step, lines):
            line_step(later, *kinds)

    rows_of = ((tok_ref, seq_ref), (cot_ref, dy_ref))

    def seat(device, half_of):
        return columns((device % QUARTERS) * 2 + half_of, rows)

    def part_seat(device, half_of, part):
        low = rows // 4 * 3
        start = ((device % QUARTERS) * 2 + half_of) * rows + part * low
        size = rows - low if part else low
        return pl.ds(pl.multiple_of(start, rows // 4), size)

    def relay(which, number, place, peer):
        view = rows_of[which][1].at[place, :]
        return remote(view, view, team_send.at[which, number], team_recv.at[which, number], peer)

    def offer(which, number, peer):
        src, dst = rows_of[which]
        return remote(
            src,
            dst.at[seat(dp, mp), :],
            team_send.at[which, number],
            team_recv.at[which, number],
            peer,
        )

    own_rows = [
        pltpu.make_async_copy(src, dst.at[seat(dp, mp), :], local_sem.at[7 + which])
        for which, (src, dst) in enumerate(rows_of)
    ]
    near, beside = seat(dp ^ 2, mp), seat(dp, other)

    far_seats = [part_seat(dp ^ 2, other, part) for part in (0, 1)]
    twin_far = [part_seat(dp ^ 3, other, part) for part in (0, 1)]
    arrivals = (near, beside, seat(dp ^ 1, mp), far_seats[0], seat(dp ^ 3, mp), far_seats[1])
    arrivals += (seat(dp ^ 1, other),) + tuple(twin_far)

    def send_rows(which, *numbers):
        for number in numbers:
            if number < 3:
                copy = offer(which, number, (across, aside, twin)[number])
            elif number in (3, 5):
                part = number // 5
                place = part_seat(dp, other, 1) if part else part_seat(dp ^ 2, mp, 0)
                copy = relay(which, number, place, across if part else aside)
            else:
                place = {4: near, 6: beside, 7: far_seats[0], 8: far_seats[1]}[number]
                copy = relay(which, number, place, twin)
            begin(copy)
            wait = relay(which, number, arrivals[number], twin).wait_recv
            expected["rows", which, number] = wait

    def pass_on(which):
        arrive("rows", which, 0)
        send_rows(which, 3, 4)
        arrive("rows", which, 1)
        send_rows(which, 5, 6)

    def hand_over(which):
        arrive("rows", which, 3)
        send_rows(which, 7)
        arrive("rows", which, 5)
        send_rows(which, 8)

    def all_rows(which):
        own_rows[which].wait()
        for number in (2, 4, 6, 7, 8):
            arrive("rows", which, number)

    def dot(a, b, contract):
        return lax.dot_general(a, b, (contract, ((), ())), preferred_element_type=F32)

    nn, nt, tn = ((1,), (0,)), ((1,), (1,)), ((0,), (0,))
    tile = min(256, count)

    def pipeline(body, grid, in_specs, out_specs, *refs):
        pltpu.emit_pipeline(
            body, grid=grid, in_specs=in_specs, out_specs=out_specs, _explicit_indices=True
        )(*refs)

    def row_blocks(size, columns_, place=0):
        return pl.BlockSpec((size, columns_), lambda i: (i, place))

    def fixed(shape, *place):
        return pl.BlockSpec(shape, lambda i: place or (0,) * len(shape))

    def normalize_rows():
        def body(step, rows_in, rows_out):
            unit_rows = normalize(rows_in[...].astype(F32))[0]
            rows_out[...] = (unit_rows * gain_v[...] + shift_v[...]).astype(BF16)

        pipeline(
            body,
            (count // tile,),
            [row_blocks(tile, width)],
            [row_blocks(tile, width)],
            seq_ref,
            normed_ref,
        )

    def activate():
        def body(step, rows_in, weight, act, slope):
            u = dot(rows_in[...], weight[...], nn) + up_bias_v[...]
            value, derivative = smooth_gate(u)
            act[...] = value.astype(BF16)
            slope[...] = derivative.astype(BF16)

        pipeline(
            body,
            (count // tile,),
            [row_blocks(tile, width), fixed((width, unit))],
            [row_blocks(tile, unit), row_blocks(tile, unit)],
            normed_ref,
            up_full_ref,
            act_ref,
            slope_ref,
        )

    tall_tile = min(512, width)

    def weight_grad(left, right, right_wide, kind, start=0):
        def body(step, a, b, out):
            out[...] = dot(a[...], b[...], tn).astype(BF16)

        pipeline(
            body,
            (width // tall_tile,),
            [
                pl.BlockSpec((count, tall_tile), lambda i: (0, i)),
                fixed((count, right_wide)),
            ],
            [row_blocks(tall_tile, right_wide)],
            left,
            right,
            grads_ref.at[kind, :, pl.ds(start, right_wide)],
        )

    def attend(hooks):
        def body(step, rows_in, dys, weight, mixed, proj):
            for number, hook in hooks.items():
                when(step.index[0] == min(number, count // length - 1), hook)
            pre = dot(rows_in[...], weight[:, : 3 * wide], nn) + in_bias_v[...]
            douts = dot(dys[...], weight[:, 3 * wide :], nn).astype(BF16)
            value, backs = attention_block(
                [pre[:, k * wide : (k + 1) * wide] for k in range(3)],
                [table_ref[k] for k in range(3)],
                douts,
            )
            mixed[...] = value
            for k in range(3):
                proj[:, k * wide : (k + 1) * wide] = backs[k]
                part = jnp.sum(backs[k].astype(F32), axis=0, keepdims=True)
                place = slice(k * wide, (k + 1) * wide)

                proj_sum_ref[:, place] = proj_sum_ref[:, place] + part

        pipeline(
            body,
            (count // length,),
            [row_blocks(length, width), row_blocks(length, width), fixed((width, 4 * wide))],
            [row_blocks(length, wide), row_blocks(length, 3 * wide)],
            normed_ref,
            dy_ref,
            heads_ref,
            mixed_ref,
            proj_ref,
        )

    def gate_back():
        def body(step, dys, weight, slope, pre):
            value = (dot(dys[...], weight[...], nn) * slope[...].astype(F32)).astype(BF16)
            pre[...] = value
            part = jnp.sum(value.astype(F32), axis=0, keepdims=True)

            @pl.when(step.index[0] == 0)
            def _():
                pre_sum_ref[...] = part

            @pl.when(step.index[0] > 0)
            def _():
                pre_sum_ref[...] = pre_sum_ref[...] + part

        pipeline(
            body,
            (count // tile,),
            [row_blocks(tile, width), fixed((width, unit)), row_blocks(tile, unit)],
            [row_blocks(tile, unit)],
            dy_ref,
            down_full_ref,
            slope_ref,
            pre_ref,
        )

    def back_to_rows(which, wide_rows, wide_weight, thin_rows, thin_wide, start, half_of, got):
        per = length // tile
        grid = (QUARTERS // 2 * per,)

        def rows_at(i):
            return ((i // per) * 2 + half_of) * per + i % per

        def body(step, a, weight, b, thin, *rest):
            sums = dot(a[...], weight[...], nt) + dot(b[...], thin[...], nt)
            if got:
                sums = sums + rest[0][...].astype(F32)
            rest[-1][...] = sums.astype(BF16)

        in_specs = [
            pl.BlockSpec((tile, unit), lambda i: (rows_at(i), 0)),
            fixed((width, unit)),
            pl.BlockSpec((tile, thin_wide), lambda i: (rows_at(i), 0)),
            fixed((width, thin_wide)),
        ]
        refs = [wide_rows, wide_weight, thin_rows, heads_ref.at[:, pl.ds(start, thin_wide)]]
        if got:
            in_specs.append(row_blocks(tile, width))
            refs.append(twin_ref.at[which])
        refs.append(pair_ref.at[which] if got else half_ref.at[which])
        pipeline(body, grid, in_specs, [row_blocks(tile, width)], *refs)

    def forward_rows(half_of, got):
        back_to_rows(0, act_ref, down_full_ref, mixed_ref, wide, 3 * wide, half_of, got)

    def backward_rows(half_of, got):
        back_to_rows(1, pre_ref, up_full_ref, proj_ref, 3 * wide, 0, half_of, got)

    def twin_copy(which):
        return remote(
            half_ref.at[which], twin_ref.at[which], twin_send.at[which], twin_recv.at[which], twin
        )

    def to_twin(which):
        begin(twin_copy(which))
        expected["twin", which] = twin_copy(which).wait_recv

    def owner_copy(which, number, peer, place):
        return remote(
            pair_ref.at[which, columns(place, rows), :],
            owner_ref.at[which, number],
            owner_send.at[which, number],
            owner_recv.at[which, number],
            peer,
        )

    chip = (dp // 2) % (QUARTERS // 2)

    def to_owners(which):
        begin(
            owner_copy(which, 2, (dp ^ 2, other), (1 - chip) * 2 + other),
            owner_copy(which, 0, across, (1 - chip) * 2 + mp),
            owner_copy(which, 1, aside, chip * 2 + other),
        )

        def wait():
            for number, peer in ((0, across), (1, aside), (2, (dp ^ 2, other))):
                owner_copy(which, number, peer, 0).wait_recv()

        expected["owner", which] = wait

    add_tile = min(256, chunk)

    def add_chunks(dst, *parts):
        def body(step, *refs):
            *ins, out = refs
            out[...] = sum(ref[...].astype(F32) for ref in ins).astype(BF16)

        pipeline(
            body,
            (chunk // add_tile,),
            [row_blocks(add_tile, unit)] * len(parts),
            [row_blocks(add_tile, unit)],
            *parts,
            dst,
        )

    def sum_sends(way, step):
        far = lines - step
        if way == 0:
            return (line <= step - 1) & has_above, line + far, line == 0
        return (line >= lines - step) & has_below, line - far, line == lines - 1

    def sum_takes(way, step):
        if way == 0:
            return has_below & (line <= step)
        return has_above & (line >= lines - 1 - step)

    def sum_copy(kind, way, step, src):
        return remote(
            src,
            land_ref.at[kind, way, step - 1],
            sum_send.at[kind, way, step - 1],
            sum_recv.at[kind, way, step - 1],
            (dp + (QUARTERS if way == 0 else -QUARTERS), mp),
        )

    def sum_start(kind, step):
        if step >= lines:
            return
        for way in (0, 1):
            go, index, first = sum_sends(way, step)
            view = grads_ref.at[kind, columns(index, chunk), :]
            staged = stage_ref.at[kind, way, step - 1]
            when(go & first, sum_copy(kind, way, step, view).start)
            if step > 1:

                def pass_on_sum():
                    add_chunks(staged, view, land_ref.at[kind, way, step - 2])
                    sum_copy(kind, way, step, staged).start()

                when(go & ~first, pass_on_sum)

        def left():
            for way in (0, 1):
                staged = stage_ref.at[kind, way, step - 1]
                when(sum_sends(way, step)[0], sum_copy(kind, way, step, staged).wait_send)

        pending.append(left)

        def wait():
            for way in (0, 1):
                staged = stage_ref.at[kind, way, step - 1]
                when(sum_takes(way, step), sum_copy(kind, way, step, staged).wait_recv)

        expected["sum", kind, step] = wait

    def sum_wait(kind, step):
        if step < lines:
            arrive("sum", kind, step)

    def sum_step(kind, step):
        sum_wait(kind, step)
        sum_start(kind, step + 1)

    def final_views(kind, of, by):
        mine = columns(of, depth)
        if kind == 1:
            views = [
                (
                    total_ref.at[1, mine, pl.ds(k * wide, wide)],
                    final_in_ref.at[k, :, columns(by, wide)],
                )
                for k in range(3)
            ]
            views.append(
                (total_ref.at[1, mine, pl.ds(3 * wide, wide)], final_out_ref.at[:, columns(by, wide)])
            )
            return views
        whole = final_down_ref if kind == 0 else final_up_ref
        return [(total_ref.at[kind, mine, :], whole.at[:, columns(by, unit)])]

    def final_copies(kind, of, by, j):
        return [
            remote(
                src,
                dst,
                final_send.at[kind, number, j - 1],
                final_recv.at[kind, number, j - 1],
                (dp ^ j, mp),
            )
            for number, (src, dst) in enumerate(final_views(kind, of, by))
        ]

    def final_own(kind):
        return [
            pltpu.make_async_copy(src, dst, local_sem.at[10 + 4 * kind + number])
            for number, (src, dst) in enumerate(final_views(kind, quarter, quarter))
        ]

    def sum_total(kind, step):
        for later in range(step, lines):
            sum_step(kind, later)
        view = grads_ref.at[kind, columns(line, chunk), :]
        below = land_ref.at[kind, 0, lines - 2]
        above = land_ref.at[kind, 1, lines - 2]

        @pl.when(has_below & has_above)
        def _():
            add_chunks(total_ref.at[kind], view, below, above)

        @pl.when(has_below & ~has_above)
        def _():
            add_chunks(total_ref.at[kind], view, below)

        @pl.when(has_above & ~has_below)
        def _():
            add_chunks(total_ref.at[kind], view, above)

        for j in (2, 3, 1):
            begin(*final_copies(kind, quarter ^ j, quarter, j))
        for copy in final_own(kind):
            copy.start()

        def wait():
            for copy in final_own(kind):
                copy.wait()
            for j in (1, 2, 3):
                for copy in final_copies(kind, quarter, quarter ^ j, j):
                    copy.wait_recv()

        expected["final", kind] = wait

    own_tile = min(64, rows)

    def own_pipeline(body, which, extra, out):
        own_place = pl.ds(pl.multiple_of((chip * 2 + mp) * rows, rows), rows)
        pipeline(
            body,
            (rows // own_tile,),
            [row_blocks(own_tile, width)] * (4 + len(extra)),
            [row_blocks(own_tile, width)],
            pair_ref.at[which, own_place, :],
            owner_ref.at[which, 0],
            owner_ref.at[which, 1],
            owner_ref.at[which, 2],
            *extra,
            out,
        )

    def add_four(parts):
        return sum(ref[...].astype(F32) for ref in parts)

    def finish_result():
        def body(step, a, b, c, d, tok, out):
            value = tok[...].astype(F32) + add_four((a, b, c, d)) + out_bias_v[...]
            out[...] = value.astype(BF16)

        own_pipeline(body, 0, [tok_ref], result_ref)

    def finish_grad():
        gain_sum[...] = jnp.zeros_like(gain_sum)
        shift_sum[...] = jnp.zeros_like(shift_sum)
        dy_sum[...] = jnp.zeros_like(dy_sum)

        def body(step, a, b, c, d, tok, cot, out):
            grad = add_four((a, b, c, d))
            unit_rows, inv_spread = normalize(tok[...].astype(F32))
            dy = cot[...].astype(F32)
            along = grad * unit_rows
            gain_sum[...] = gain_sum[...] + jnp.sum(along, axis=0, keepdims=True)
            shift_sum[...] = shift_sum[...] + jnp.sum(grad, axis=0, keepdims=True)
            dy_sum[...] = dy_sum[...] + jnp.sum(dy, axis=0, keepdims=True)
            scaled = grad * gain_v[...]
            centered = (
                scaled
                - jnp.mean(scaled, axis=-1, keepdims=True)
                - unit_rows * jnp.mean(along * gain_v[...], axis=-1, keepdims=True)
            )
            out[...] = dy + inv_spread * centered

        own_pipeline(body, 1, [tok_ref, cot_ref], grad_ref)

    def small_move(number, src, dst, peer):
        return remote(src, dst, small_send.at[number], small_recv.at[number], peer)

    def sum_small():
        vector[...] = jnp.zeros_like(vector)
        for l in range(lines):
            for q in range(QUARTERS):
                d = l * QUARTERS + q
                place = slice(d * each, (d + 1) * each)
                for number, ref in enumerate((gain_sum, shift_sum, dy_sum)):
                    vector[q, l, number : number + 1, :each] = ref[:, place]
        for i in range(lines):
            owner = quarter * lines + i
            q, l = owner % QUARTERS, owner // QUARTERS
            for k in range(3):
                start = k * wide + i * in_each
                vector[q, l, 3 + k : 4 + k, :in_each] = proj_sum_ref[:, start : start + in_each]
            for r in range(up_each // up_low):
                start = i * up_each + r * up_low
                vector[q, l, 6 + r : 7 + r, :up_low] = pre_sum_ref[:, start : start + up_low]
        first = [
            small_move(j - 1, vector.at[quarter ^ j], vector_land.at[j - 1], (dp ^ j, mp))
            for j in (1, 2, 3)
        ]
        for copy in first:
            copy.start()
        for copy in first:
            copy.wait()
        part[...] = (vector[quarter] + vector_land[0]) + (vector_land[1] + vector_land[2])
        second = [
            small_move(
                2 + k, part.at[lax.rem(line + k, lines)], part_land.at[k - 1], in_line(k)
            )
            for k in range(1, lines)
        ]
        for copy in second:
            copy.start()
        total = part[line]
        for k, copy in enumerate(second):
            copy.wait()
            total = total + part_land[k]
        own_small_ref[...] = total
        third = small_move(2 + lines, own_small_ref, aside_land, aside)
        third.start()
        third.wait()
        row = lax.broadcasted_iota(jnp.int32, total.shape, 0)
        own_small_ref[...] = jnp.where(row < 3, total + aside_land[...], total)

    begin_swap(0, 1)
    send_rows(0, 1, 2)
    own_rows[0].start()
    own_rows[1].start()
    end_swap(0, 1)
    start_line(1, 0, 1)
    begin_swap(2, 3, 4, 5)
    send_rows(0, 0)
    line_step(1, 0, 1)
    pass_on(0)
    end_swap(2, 3, 4, 5)
    start_line(1, 2)
    hand_over(0)
    send_rows(1, 1, 2)
    send_rows(1, 0)
    line_step(2, 0, 1)
    begin_swap(6)
    all_rows(0)
    line_rest(3, 0)
    fetch = pltpu.make_async_copy(smalls_ref, small_v, local_sem.at[9])
    fetch.start()
    fetch.wait()
    small_f[...] = small_v[...].astype(F32)
    for d in range(lines * QUARTERS):
        place = slice(d * each, (d + 1) * each)
        gain_v[:, place] = small_f[d * tall : d * tall + 1, :each]
        shift_v[:, place] = small_f[d * tall + 1 : d * tall + 2, :each]
        bias = small_f[d * tall + 2 : d * tall + 3, :each]
        out_bias_v[:, place] = bias + small_f[d * tall + 3 : d * tall + 4, :each]
    for i in range(lines):
        top = pl.multiple_of((quarter * lines + i) * tall, tall)
        block = small_f[pl.ds(top, tall), :]
        for k in range(3):
            start = k * wide + i * in_each
            in_bias_v[:, start : start + in_each] = block[4 + k : 5 + k, :in_each]
        for r in range(up_each // up_low):
            start = i * up_each + r * up_low
            up_bias_v[:, start : start + up_low] = block[7 + r : 8 + r, :up_low]
    normalize_rows()
    line_step(1, 2)
    pass_on(1)
    line_rest(3, 1)
    activate()
    hand_over(1)
    line_step(2, 2)
    end_swap(6)
    start_line(1, 3)
    all_rows(1)
    weight_grad(dy_ref, act_ref, unit, 0)
    sum_start(0, 1)
    line_rest(3, 2)
    proj_sum_ref[...] = jnp.zeros_like(proj_sum_ref)
    attend({2: lambda: line_step(1, 3), 3: lambda: sum_step(0, 1)})
    line_step(2, 3)
    weight_grad(dy_ref, mixed_ref, wide, 1, 3 * wide)
    weight_grad(normed_ref, proj_ref, 3 * wide, 1, 0)
    sum_step(0, 2)
    line_rest(3, 3)
    sum_start(1, 1)
    forward_rows(1 - core, False)
    to_twin(0)
    gate_back()
    weight_grad(normed_ref, pre_ref, unit, 2)
    sum_start(2, 1)
    sum_total(0, 3)
    arrive("twin", 0)
    forward_rows(core, True)
    to_owners(0)
    sum_step(1, 1)
    backward_rows(1 - core, False)
    to_twin(1)
    sum_step(2, 1)
    arrive("twin", 1)
    backward_rows(core, True)
    to_owners(1)
    sum_step(1, 2)
    sum_step(2, 2)
    sum_total(1, 3)
    arrive("owner", 0)
    finish_result()
    arrive("owner", 1)
    finish_grad()
    sum_total(2, 3)
    sum_small()

    for key in list(expected):
        arrive(*key)
    for wait in pending:
        wait()


def run_layer(lines, team, tokens, cotangent, in_weight, out_weight, up_weight, down_weight, small, table):
    rows, width = tokens.shape
    depth = out_weight.shape[0]
    wide = out_weight.shape[1] // QUARTERS
    unit = up_weight.shape[1] // QUARTERS
    chunk = QUARTERS * depth
    whole = lines * chunk
    count = team * rows
    smalls = lines * QUARTERS * small.shape[0]
    steps = max(lines - 1, 1)
    anywhere = pl.BlockSpec(memory_space=pl.ANY)
    inside = pl.BlockSpec(memory_space=pltpu.VMEM)

    def low(*shape):
        return jax.ShapeDtypeStruct(shape, BF16)

    outs = [
        low(count, width),
        low(count, width),
        low(whole, 4 * wide),
        low(whole, unit),
        low(whole, unit),
        low(smalls, 128),
        low(count, width),
        low(count, unit),
        low(count, unit),
        low(count, wide),
        low(count, 3 * wide),
        low(count, unit),
        low(3, width, unit),
        low(3, 2, steps, chunk, unit),
        low(3, 2, steps, chunk, unit),
        low(3, chunk, unit),
        low(2, count // 2, width),
        low(2, count // 2, width),
        low(2, count // 2, width),
        low(2, 3, rows, width),
        low(rows, width),
        jax.ShapeDtypeStruct((rows, width), F32),
        low(depth, QUARTERS * unit),
        low(depth, QUARTERS * unit),
        low(3, depth, QUARTERS * wide),
        low(depth, QUARTERS * wide),
    ]
    tile = (8, 128)
    dma = pltpu.SemaphoreType.DMA
    results = pl.pallas_call(
        functools.partial(layer_kernel, lines),
        out_shape=outs + [jax.ShapeDtypeStruct(tile, F32)],
        in_specs=[anywhere] * 7 + [inside],
        out_specs=[anywhere] * len(outs) + [inside],
        scratch_shapes=[
            pltpu.VMEM((1, 3 * wide), F32),
            pltpu.VMEM((1, unit), F32),
            pltpu.VMEM((1, width), F32),
            pltpu.VMEM((1, width), F32),
            pltpu.VMEM((1, width), F32),
            pltpu.VMEM((QUARTERS, lines) + tile, F32),
            pltpu.VMEM((3, lines) + tile, F32),
            pltpu.VMEM((lines,) + tile, F32),
            pltpu.VMEM((steps,) + tile, F32),
            pltpu.VMEM(tile, F32),
            pltpu.VMEM((smalls, 128), BF16),
            pltpu.VMEM((smalls, 128), F32),
            pltpu.VMEM((1, width), F32),
            pltpu.VMEM((1, width), F32),
            pltpu.VMEM((1, width), F32),
            pltpu.VMEM((1, 3 * wide), F32),
            pltpu.VMEM((1, unit), F32),
            dma((22,)),
            dma((7, 3)),
            dma((7, 3)),
            dma((2, 9)),
            dma((2, 9)),
            dma((4, 2, steps)),
            dma((4, 2, steps)),
            dma((3, 2, steps)),
            dma((3, 2, steps)),
            dma((3, 4, 3)),
            dma((3, 4, 3)),
            dma((2,)),
            dma((2,)),
            dma((2, 3)),
            dma((2, 3)),
            dma((lines + 3,)),
            dma((lines + 3,)),
        ],
        compiler_params=pltpu.CompilerParams(
            collective_id=1, has_side_effects=True, vmem_limit_bytes=VMEM_BYTES
        ),
    )(tokens, cotangent, in_weight, out_weight, up_weight, down_weight, small, table)
    return results[20:]


def smooth_gate(u):
    slope = math.sqrt(2.0 / math.pi)
    square = u * u
    curve = jnp.tanh(slope * (u + 0.044715 * (u * square)))
    rise = 0.5 * (1.0 + curve)
    bend = 0.5 * u * (1.0 - curve * curve) * (slope * (1.0 + 3.0 * 0.044715 * square))
    return u * rise, rise + bend


def per_device(
    tokens,
    norm_gain,
    norm_shift,
    in_weight,
    in_bias,
    out_weight,
    out_bias,
    up_weight,
    up_bias,
    down_weight,
    down_bias,
    cotangent,
):
    n_dp = lax.axis_size("dp")
    n_mp = lax.axis_size("mp")
    lines = n_dp // QUARTERS
    own_rows, width = tokens.shape
    each = norm_gain.shape[0]
    in_each = in_bias.shape[1]
    up_each = up_bias.shape[0]
    wide = out_weight.shape[1] // QUARTERS

    def row(vector):
        return jnp.pad(vector, (0, -vector.shape[0] % 128)).reshape(-1, 128)

    small = jnp.concatenate(
        [row(norm_gain), row(norm_shift), row(out_bias), row(down_bias)]
        + [row(in_bias[k]) for k in range(3)]
        + [row(up_bias)]
    )
    small = jnp.pad(small, ((0, SMALL - small.shape[0]), (0, 0)))
    table = rotary_tables(n_mp * own_rows, wide // HEAD)
    outcome, grad_input, grad_down, grad_up, grad_in, grad_out, owned = run_layer(
        lines, QUARTERS * n_mp, tokens, cotangent, in_weight, out_weight, up_weight, down_weight, small, table
    )
    own_bias = owned[2, :each]
    return (
        outcome,
        grad_input,
        owned[0, :each],
        owned[1, :each],
        grad_in.astype(F32),
        owned[3:6, :in_each],
        grad_out.astype(F32),
        own_bias,
        grad_up.astype(F32),
        owned[6:8, : min(up_each, 128)].reshape(-1)[:up_each],
        grad_down.astype(F32),
        own_bias,
    )


def solution(mesh):
    return jax.shard_map(
        per_device,
        mesh=mesh,
        in_specs=(
            P(("dp", "mp"), None),
            P("dp"),
            P("dp"),
            P(None, "dp", "mp"),
            P(None, ("mp", "dp")),
            P("dp", "mp"),
            P("dp"),
            P("dp", "mp"),
            P(("mp", "dp")),
            P("dp", "mp"),
            P("dp"),
            P(("dp", "mp"), None),
        ),
        out_specs=(
            P(("dp", "mp"), None),
            P(("dp", "mp"), None),
            P("dp"),
            P("dp"),
            P(None, "dp", "mp"),
            P(None, ("mp", "dp")),
            P("dp", "mp"),
            P("dp"),
            P("dp", "mp"),
            P(("mp", "dp")),
            P("dp", "mp"),
            P("dp"),
        ),
        check_vma=False,
    )
```

```python
import functools
import math

import jax
import jax.numpy as jnp
import numpy as np
from jax import lax
from jax.experimental import pallas as pl
from jax.experimental.pallas import tpu as pltpu
from jax.sharding import PartitionSpec as P

HEAD = 64
ROT = 32
QUARTERS = 4
SMALL = 16
norm_eps = 1e-05
F32 = jnp.float32
BF16 = jnp.bfloat16


def normalize(rows):
    middle = jnp.mean(rows, axis=-1, keepdims=True)
    centered = rows - middle
    spread = jnp.mean(centered * centered, axis=-1, keepdims=True)
    inv_spread = lax.rsqrt(spread + norm_eps)
    return (centered * inv_spread, inv_spread)


def roll_lanes(v, by):
    return pltpu.roll(v, by, 1)


def attention_block(pre, table, douts):
    length, wide = douts.shape
    heads = wide // HEAD
    block = length // 2
    half_rot = ROT // 2
    scale = 1.0 / math.sqrt(HEAD)
    cosine, first, second = table

    def turn(v):
        return (
            v * cosine
            + roll_lanes(v, wide - half_rot) * first
            + roll_lanes(v, half_rot) * second
        )

    def turn_back(g):
        return (
            g * cosine
            + roll_lanes(g * first, half_rot)
            + roll_lanes(g * second, wide - half_rot)
        )

    queries = turn(pre[0]).astype(BF16)
    keys = turn(pre[1]).astype(BF16)
    values = pre[2].astype(BF16)
    head_of = lax.broadcasted_iota(jnp.int32, (block, wide), 1) // HEAD
    nothing = jnp.zeros((block, wide), BF16)
    mixed = [None, None]
    dq, dk, dv = [None, None], [None, None], [None, None]

    def dot(a, b, contract):
        return lax.dot_general(a, b, (contract, ((), ())), preferred_element_type=F32)

    def add(total, part):
        return part if total is None else total + part

    for head in range(heads):
        here = head_of == head

        def only(v):
            return jnp.where(here, v, nothing)

        q_here = [only(queries[i * block : (i + 1) * block]) for i in range(2)]
        k_here = [only(keys[i * block : (i + 1) * block]) for i in range(2)]
        v_here = [only(values[i * block : (i + 1) * block]) for i in range(2)]
        d_here = [only(douts[i * block : (i + 1) * block]) for i in range(2)]
        for i in range(2):
            seen = (i + 1) * block
            scores = dot(q_here[i], keys[:seen], ((1,), (1,))) * scale
            row = lax.broadcasted_iota(jnp.int32, (block, seen), 0) + i * block
            col = lax.broadcasted_iota(jnp.int32, (block, seen), 1)
            scores = jnp.where(col <= row, scores, -1e30)
            powers = jnp.exp(scores - jnp.max(scores, axis=1, keepdims=True))
            probs = powers * (1.0 / jnp.sum(powers, axis=1, keepdims=True))
            low = probs.astype(BF16)
            dprobs = dot(d_here[i], values[:seen], ((1,), (1,)))
            total = jnp.sum(probs * dprobs, axis=1, keepdims=True)
            dscores = (probs * (dprobs - total)).astype(BF16)
            for j in range(i + 1):
                part = slice(j * block, (j + 1) * block)
                mixed[i] = add(mixed[i], dot(low[:, part], v_here[j], ((1,), (0,))))
                dq[i] = add(dq[i], dot(dscores[:, part], k_here[j], ((1,), (0,))))
                dv[j] = add(dv[j], dot(low[:, part], d_here[i], ((0,), (0,))))
                dk[j] = add(dk[j], dot(dscores[:, part], q_here[i], ((0,), (0,))))
    value = jnp.concatenate(mixed, axis=0).astype(BF16)
    dq_low = (jnp.concatenate(dq, axis=0) * scale).astype(BF16)
    dk_low = (jnp.concatenate(dk, axis=0) * scale).astype(BF16)
    backs = (
        turn_back(dq_low.astype(F32)).astype(BF16),
        turn_back(dk_low.astype(F32)).astype(BF16),
        jnp.concatenate(dv, axis=0).astype(BF16),
    )
    return value, backs


def rotary_tables(length, heads):
    half_rot = ROT // 2
    freqs = np.exp(np.arange(half_rot) * (-math.log(10000.0) / half_rot))
    angles = np.arange(length)[:, None] * freqs[None, :]
    cosine, sine = np.cos(angles), np.sin(angles)
    rest = np.zeros((length, HEAD - ROT))
    none = np.zeros_like(sine)
    tables = np.stack(
        [
            np.concatenate([cosine, cosine, rest + 1.0], axis=1),
            np.concatenate([-sine, none, rest], axis=1),
            np.concatenate([none, sine, rest], axis=1),
        ]
    )
    return jnp.asarray(np.tile(tables, (1, 1, heads)), F32)


MESH = pl.DeviceIdType.MESH
VMEM_BYTES = 60 * 2**20


def layer_kernel(
    lines,
    tok_ref,
    cot_ref,
    in_ref,
    out_ref,
    up_ref,
    down_ref,
    small_ref,
    table_ref,
    seq_ref,
    dy_ref,
    heads_ref,
    up_full_ref,
    down_full_ref,
    smalls_ref,
    normed_ref,
    act_ref,
    slope_ref,
    mixed_ref,
    proj_ref,
    pre_ref,
    grads_ref,
    land_ref,
    stage_ref,
    total_ref,
    half_ref,
    twin_ref,
    pair_ref,
    owner_ref,
    result_ref,
    grad_ref,
    final_down_ref,
    final_up_ref,
    final_in_ref,
    final_out_ref,
    own_small_ref,
    proj_sum_ref,
    pre_sum_ref,
    gain_sum,
    shift_sum,
    dy_sum,
    vector,
    vector_land,
    part,
    part_land,
    aside_land,
    small_v,
    small_f,
    gain_v,
    shift_v,
    out_bias_v,
    in_bias_v,
    up_bias_v,
    local_sem,
    swap_send,
    swap_recv,
    team_send,
    team_recv,
    line_send,
    line_recv,
    sum_send,
    sum_recv,
    final_send,
    final_recv,
    twin_send,
    twin_recv,
    owner_send,
    owner_recv,
    small_send,
    small_recv,
):
    dp = lax.axis_index("dp")
    mp = lax.axis_index("mp")
    quarter = dp % QUARTERS
    line = dp // QUARTERS
    other = 1 - mp
    core = dp % 2
    rows, width = tok_ref.shape
    depth = out_ref.shape[0]
    chunk = QUARTERS * depth
    wide = out_ref.shape[1] // QUARTERS
    unit = up_ref.shape[1] // QUARTERS
    tall = small_ref.shape[0]
    length = table_ref.shape[1]
    count = seq_ref.shape[0]
    each = width // (lines * QUARTERS)
    in_each = wide // lines
    up_each = unit // lines
    up_low = min(up_each, 128)
    has_above = line < lines - 1
    has_below = line > 0
    across, aside, twin = (dp ^ 2, mp), (dp, other), (dp ^ 1, mp)

    barrier = pltpu.get_barrier_semaphore()
    def in_line(k):
        return (lax.rem(line + k, lines) * QUARTERS + quarter, mp)

    peers = [twin, across, (dp ^ 3, mp), aside, (dp ^ 2, other)]
    peers += [in_line(k) for k in range(1, lines)]
    for peer in peers:
        pl.semaphore_signal(barrier, inc=1, device_id=peer, device_id_type=MESH)
    pl.semaphore_wait(barrier, len(peers))

    pending = []
    expected = {}

    def begin(make):
        for copy in make():
            copy.start()

        def left():
            for copy in make():
                copy.wait_send()

        pending.append(left)

    def arrive(*key):
        expected.pop(key)()

    def remote(src, dst, send, recv, peer):
        return pltpu.make_async_remote_copy(
            src_ref=src,
            dst_ref=dst,
            send_sem=send,
            recv_sem=recv,
            device_id=peer,
            device_id_type=MESH,
        )

    def columns(index, size):
        return pl.ds(pl.multiple_of(index * size, size), size)

    def weight_views(device, to):
        mine, part = columns(device, depth), columns(device, depth)
        views = [
            (small_ref, smalls_ref.at[columns(device, tall), :]),
            (up_ref.at[:, columns(to, unit)], up_full_ref.at[mine, :]),
        ]
        for k in range(3):
            views.append(
                (in_ref.at[k, :, columns(to, wide)], heads_ref.at[part, pl.ds(k * wide, wide)])
            )
        views.append((out_ref.at[:, columns(to, wide)], heads_ref.at[part, pl.ds(3 * wide, wide)]))
        views.append((down_ref.at[:, columns(to, unit)], down_full_ref.at[part, :]))
        return views

    def swap(kind, j, device):
        src, dst = weight_views(device, quarter ^ j)[kind]
        return remote(
            src, dst, swap_send.at[kind, j - 1], swap_recv.at[kind, j - 1], (dp ^ j, mp)
        )

    own = [
        pltpu.make_async_copy(src, dst, local_sem.at[kind])
        for kind, (src, dst) in enumerate(weight_views(dp, quarter))
    ]

    def begin_swap(*kinds):
        for kind in kinds:
            begin(lambda kind=kind: [swap(kind, j, dp) for j in (2, 3, 1)])
            own[kind].start()

            def wait(kind=kind):
                own[kind].wait()
                for j in (1, 2, 3):
                    swap(kind, j, dp ^ j).wait_recv()

            expected["swap", kind] = wait

    def end_swap(*kinds):
        for kind in kinds:
            arrive("swap", kind)

    def line_view(kind, index):
        if kind == 0:
            return smalls_ref.at[columns(index, QUARTERS * tall), :]
        return (up_full_ref, heads_ref, down_full_ref)[kind - 1].at[columns(index, chunk), :]

    def line_copy(kind, way, step, index):
        view = line_view(kind, index)
        return remote(
            view,
            view,
            line_send.at[kind, way, step - 1],
            line_recv.at[kind, way, step - 1],
            (dp + (QUARTERS if way == 0 else -QUARTERS), mp),
        )

    def sends(way, step):
        if way == 0:
            return (line >= step - 1) & has_above, line - (step - 1)
        return (line <= lines - step) & has_below, line + (step - 1)

    def takes(way, step):
        if way == 0:
            return line >= step, line - step
        return line <= lines - 1 - step, line + step

    def when(go, act):
        @pl.when(go)
        def _():
            act()

    def start_line(step, *kinds):
        if step < lines:
            for kind in kinds:
                for way in (0, 1):
                    go, index = sends(way, step)
                    copy = line_copy(kind, way, step, index)
                    when(go, copy.start)

                def left(kind=kind):
                    for way in (0, 1):
                        go, index = sends(way, step)
                        when(go, line_copy(kind, way, step, index).wait_send)

                pending.append(left)

                def wait(kind=kind):
                    for way in (0, 1):
                        go, index = takes(way, step)
                        when(go, line_copy(kind, way, step, index).wait_recv)

                expected["line", kind, step] = wait

    def wait_line(step, *kinds):
        if step < lines:
            for kind in kinds:
                arrive("line", kind, step)

    def line_step(step, *kinds):
        wait_line(step, *kinds)
        start_line(step + 1, *kinds)

    def line_rest(step, *kinds):
        for later in range(step, lines):
            line_step(later, *kinds)

    rows_of = ((tok_ref, seq_ref), (cot_ref, dy_ref))

    def seat(device, half_of):
        return columns((device % QUARTERS) * 2 + half_of, rows)

    def part_seat(device, half_of, part):
        low = rows // 4 * 3
        start = ((device % QUARTERS) * 2 + half_of) * rows + part * low
        size = rows - low if part else low
        return pl.ds(pl.multiple_of(start, rows // 4), size)

    def relay(which, number, place, peer):
        view = rows_of[which][1].at[place, :]
        return remote(view, view, team_send.at[which, number], team_recv.at[which, number], peer)

    def offer(which, number, peer):
        src, dst = rows_of[which]
        return remote(
            src,
            dst.at[seat(dp, mp), :],
            team_send.at[which, number],
            team_recv.at[which, number],
            peer,
        )

    own_rows = [
        pltpu.make_async_copy(src, dst.at[seat(dp, mp), :], local_sem.at[7 + which])
        for which, (src, dst) in enumerate(rows_of)
    ]
    near, beside = seat(dp ^ 2, mp), seat(dp, other)

    far_seats = [part_seat(dp ^ 2, other, part) for part in (0, 1)]
    twin_far = [part_seat(dp ^ 3, other, part) for part in (0, 1)]
    arrivals = (near, beside, seat(dp ^ 1, mp), far_seats[0], seat(dp ^ 3, mp), far_seats[1])
    arrivals += (seat(dp ^ 1, other),) + tuple(twin_far)

    def send_rows(which, *numbers):
        def copy_of(number):
            if number < 3:
                return offer(which, number, (across, aside, twin)[number])
            if number in (3, 5):
                part = number // 5
                place = part_seat(dp, other, 1) if part else part_seat(dp ^ 2, mp, 0)
                return relay(which, number, place, across if part else aside)
            place = {4: near, 6: beside, 7: far_seats[0], 8: far_seats[1]}[number]
            return relay(which, number, place, twin)

        for number in numbers:
            begin(lambda number=number: [copy_of(number)])

            def wait(number=number):
                relay(which, number, arrivals[number], twin).wait_recv()

            expected["rows", which, number] = wait

    def pass_on(which):
        arrive("rows", which, 0)
        send_rows(which, 3, 4)
        arrive("rows", which, 1)
        send_rows(which, 5, 6)

    def hand_over(which):
        arrive("rows", which, 3)
        send_rows(which, 7)
        arrive("rows", which, 5)
        send_rows(which, 8)

    def all_rows(which):
        own_rows[which].wait()
        for number in (2, 4, 6, 7, 8):
            arrive("rows", which, number)

    def dot(a, b, contract):
        return lax.dot_general(a, b, (contract, ((), ())), preferred_element_type=F32)

    nn, nt, tn = ((1,), (0,)), ((1,), (1,)), ((0,), (0,))
    tile = min(256, count)

    def pipeline(body, grid, in_specs, out_specs, *refs):
        pltpu.emit_pipeline(
            body, grid=grid, in_specs=in_specs, out_specs=out_specs, _explicit_indices=True
        )(*refs)

    def row_blocks(size, columns_, place=0):
        return pl.BlockSpec((size, columns_), lambda i: (i, place))

    def fixed(shape, *place):
        return pl.BlockSpec(shape, lambda i: place or (0,) * len(shape))

    def normalize_rows():
        def body(step, rows_in, rows_out):
            unit_rows = normalize(rows_in[...].astype(F32))[0]
            rows_out[...] = (unit_rows * gain_v[...] + shift_v[...]).astype(BF16)

        pipeline(
            body,
            (count // tile,),
            [row_blocks(tile, width)],
            [row_blocks(tile, width)],
            seq_ref,
            normed_ref,
        )

    def activate(hooks):
        def body(step, rows_in, weight, act, slope):
            call_hooks(step, hooks, count // tile)
            u = dot(rows_in[...], weight[...], nn) + up_bias_v[...]
            value, derivative = smooth_gate(u)
            act[...] = value.astype(BF16)
            slope[...] = derivative.astype(BF16)

        pipeline(
            body,
            (count // tile,),
            [row_blocks(tile, width), fixed((width, unit))],
            [row_blocks(tile, unit), row_blocks(tile, unit)],
            normed_ref,
            up_full_ref,
            act_ref,
            slope_ref,
        )

    far_chunk = jnp.where(2 * line < lines, lines - 1, 0)

    def weight_grad(part, left, right, right_wide, kind, start=0):
        def place(i):
            return lax.rem(far_chunk + i + (0 if part == "far" else 1), lines)

        def body(step, a, b, out):
            out[...] = dot(a[...], b[...], tn).astype(BF16)

        pipeline(
            body,
            (1 if part == "far" else lines - 1,),
            [
                pl.BlockSpec((count, chunk), lambda i: (0, place(i))),
                fixed((count, right_wide)),
            ],
            [pl.BlockSpec((chunk, right_wide), lambda i: (place(i), 0))],
            left,
            right,
            grads_ref.at[kind, :, pl.ds(start, right_wide)],
        )

    def call_hooks(step, hooks, last):
        for number, hook in hooks.items():
            when(step.index[0] == min(number, last - 1), hook)

    def attend(hooks):
        def body(step, rows_in, dys, weight, mixed, proj):
            call_hooks(step, hooks, count // length)
            pre = dot(rows_in[...], weight[:, : 3 * wide], nn) + in_bias_v[...]
            douts = dot(dys[...], weight[:, 3 * wide :], nn).astype(BF16)
            value, backs = attention_block(
                [pre[:, k * wide : (k + 1) * wide] for k in range(3)],
                [table_ref[k] for k in range(3)],
                douts,
            )
            mixed[...] = value
            for k in range(3):
                proj[:, k * wide : (k + 1) * wide] = backs[k]
                part = jnp.sum(backs[k].astype(F32), axis=0, keepdims=True)
                place = slice(k * wide, (k + 1) * wide)

                proj_sum_ref[:, place] = proj_sum_ref[:, place] + part

        pipeline(
            body,
            (count // length,),
            [row_blocks(length, width), row_blocks(length, width), fixed((width, 4 * wide))],
            [row_blocks(length, wide), row_blocks(length, 3 * wide)],
            normed_ref,
            dy_ref,
            heads_ref,
            mixed_ref,
            proj_ref,
        )

    def gate_back(hooks):
        def body(step, dys, weight, slope, pre):
            call_hooks(step, hooks, count // tile)
            value = (dot(dys[...], weight[...], nn) * slope[...].astype(F32)).astype(BF16)
            pre[...] = value
            part = jnp.sum(value.astype(F32), axis=0, keepdims=True)

            @pl.when(step.index[0] == 0)
            def _():
                pre_sum_ref[...] = part

            @pl.when(step.index[0] > 0)
            def _():
                pre_sum_ref[...] = pre_sum_ref[...] + part

        pipeline(
            body,
            (count // tile,),
            [row_blocks(tile, width), fixed((width, unit)), row_blocks(tile, unit)],
            [row_blocks(tile, unit)],
            dy_ref,
            down_full_ref,
            slope_ref,
            pre_ref,
        )

    def back_to_rows(which, wide_rows, wide_weight, thin_rows, thin_wide, start, half_of, got):
        per = length // tile
        grid = (QUARTERS // 2 * per,)

        def rows_at(i):
            return ((i // per) * 2 + half_of) * per + i % per

        def body(step, a, weight, b, thin, *rest):
            sums = dot(a[...], weight[...], nt) + dot(b[...], thin[...], nt)
            if got:
                sums = sums + rest[0][...].astype(F32)
            rest[-1][...] = sums.astype(BF16)

        in_specs = [
            pl.BlockSpec((tile, unit), lambda i: (rows_at(i), 0)),
            fixed((width, unit)),
            pl.BlockSpec((tile, thin_wide), lambda i: (rows_at(i), 0)),
            fixed((width, thin_wide)),
        ]
        refs = [wide_rows, wide_weight, thin_rows, heads_ref.at[:, pl.ds(start, thin_wide)]]
        if got:
            in_specs.append(row_blocks(tile, width))
            refs.append(twin_ref.at[which])
        refs.append(pair_ref.at[which] if got else half_ref.at[which])
        pipeline(body, grid, in_specs, [row_blocks(tile, width)], *refs)

    def forward_rows(half_of, got):
        back_to_rows(0, act_ref, down_full_ref, mixed_ref, wide, 3 * wide, half_of, got)

    def backward_rows(half_of, got):
        back_to_rows(1, pre_ref, up_full_ref, proj_ref, 3 * wide, 0, half_of, got)

    def twin_copy(which):
        return remote(
            half_ref.at[which], twin_ref.at[which], twin_send.at[which], twin_recv.at[which], twin
        )

    def to_twin(which):
        begin(lambda: [twin_copy(which)])
        expected["twin", which] = lambda: twin_copy(which).wait_recv()

    def owner_copy(which, number, peer, place):
        return remote(
            pair_ref.at[which, columns(place, rows), :],
            owner_ref.at[which, number],
            owner_send.at[which, number],
            owner_recv.at[which, number],
            peer,
        )

    chip = (dp // 2) % (QUARTERS // 2)

    def to_owners(which):
        begin(
            lambda: [
                owner_copy(which, 2, (dp ^ 2, other), (1 - chip) * 2 + other),
                owner_copy(which, 0, across, (1 - chip) * 2 + mp),
                owner_copy(which, 1, aside, chip * 2 + other),
            ]
        )

        def wait():
            for number, peer in ((0, across), (1, aside), (2, (dp ^ 2, other))):
                owner_copy(which, number, peer, 0).wait_recv()

        expected["owner", which] = wait

    add_tile = min(256, chunk)

    def add_chunks(dst, *parts):
        def body(step, *refs):
            *ins, out = refs
            out[...] = sum(ref[...].astype(F32) for ref in ins).astype(BF16)

        pipeline(
            body,
            (chunk // add_tile,),
            [row_blocks(add_tile, unit)] * len(parts),
            [row_blocks(add_tile, unit)],
            *parts,
            dst,
        )

    def sum_sends(way, step):
        far = lines - step
        if way == 0:
            return (line <= step - 1) & has_above, line + far, line == 0
        return (line >= lines - step) & has_below, line - far, line == lines - 1

    def sum_takes(way, step):
        if way == 0:
            return has_below & (line <= step)
        return has_above & (line >= lines - 1 - step)

    def sum_copy(kind, way, step, src):
        return remote(
            src,
            land_ref.at[kind, way, step - 1],
            sum_send.at[kind, way, step - 1],
            sum_recv.at[kind, way, step - 1],
            (dp + (QUARTERS if way == 0 else -QUARTERS), mp),
        )

    def sum_start(kind, step):
        if step >= lines:
            return
        for way in (0, 1):
            go, index, first = sum_sends(way, step)
            view = grads_ref.at[kind, columns(index, chunk), :]
            staged = stage_ref.at[kind, way, step - 1]
            when(go & first, sum_copy(kind, way, step, view).start)
            if step > 1:

                def pass_on_sum():
                    add_chunks(staged, view, land_ref.at[kind, way, step - 2])
                    sum_copy(kind, way, step, staged).start()

                when(go & ~first, pass_on_sum)

        def left():
            for way in (0, 1):
                staged = stage_ref.at[kind, way, step - 1]
                when(sum_sends(way, step)[0], sum_copy(kind, way, step, staged).wait_send)

        pending.append(left)

        def wait():
            for way in (0, 1):
                staged = stage_ref.at[kind, way, step - 1]
                when(sum_takes(way, step), sum_copy(kind, way, step, staged).wait_recv)

        expected["sum", kind, step] = wait

    def sum_wait(kind, step):
        if step < lines:
            arrive("sum", kind, step)

    def sum_step(kind, step):
        sum_wait(kind, step)
        sum_start(kind, step + 1)

    def final_views(kind, of, by):
        mine = columns(of, depth)
        if kind == 1:
            views = [
                (
                    total_ref.at[1, mine, pl.ds(k * wide, wide)],
                    final_in_ref.at[k, :, columns(by, wide)],
                )
                for k in range(3)
            ]
            views.append(
                (total_ref.at[1, mine, pl.ds(3 * wide, wide)], final_out_ref.at[:, columns(by, wide)])
            )
            return views
        whole = final_down_ref if kind == 0 else final_up_ref
        return [(total_ref.at[kind, mine, :], whole.at[:, columns(by, unit)])]

    def final_copies(kind, of, by, j):
        return [
            remote(
                src,
                dst,
                final_send.at[kind, number, j - 1],
                final_recv.at[kind, number, j - 1],
                (dp ^ j, mp),
            )
            for number, (src, dst) in enumerate(final_views(kind, of, by))
        ]

    def final_own(kind):
        return [
            pltpu.make_async_copy(src, dst, local_sem.at[10 + 4 * kind + number])
            for number, (src, dst) in enumerate(final_views(kind, quarter, quarter))
        ]

    def sum_total(kind, step):
        for later in range(step, lines):
            sum_step(kind, later)
        view = grads_ref.at[kind, columns(line, chunk), :]
        below = land_ref.at[kind, 0, lines - 2]
        above = land_ref.at[kind, 1, lines - 2]

        @pl.when(has_below & has_above)
        def _():
            add_chunks(total_ref.at[kind], view, below, above)

        @pl.when(has_below & ~has_above)
        def _():
            add_chunks(total_ref.at[kind], view, below)

        @pl.when(has_above & ~has_below)
        def _():
            add_chunks(total_ref.at[kind], view, above)

        begin(
            lambda: [
                copy for j in (2, 3, 1) for copy in final_copies(kind, quarter ^ j, quarter, j)
            ]
        )
        for copy in final_own(kind):
            copy.start()

        def wait():
            for copy in final_own(kind):
                copy.wait()
            for j in (1, 2, 3):
                for copy in final_copies(kind, quarter, quarter ^ j, j):
                    copy.wait_recv()

        expected["final", kind] = wait

    own_tile = min(64, rows)

    def own_pipeline(body, which, extra, out):
        own_place = pl.ds(pl.multiple_of((chip * 2 + mp) * rows, rows), rows)
        pipeline(
            body,
            (rows // own_tile,),
            [row_blocks(own_tile, width)] * (4 + len(extra)),
            [row_blocks(own_tile, width)],
            pair_ref.at[which, own_place, :],
            owner_ref.at[which, 0],
            owner_ref.at[which, 1],
            owner_ref.at[which, 2],
            *extra,
            out,
        )

    def add_four(parts):
        return sum(ref[...].astype(F32) for ref in parts)

    def finish_result():
        def body(step, a, b, c, d, tok, out):
            value = tok[...].astype(F32) + add_four((a, b, c, d)) + out_bias_v[...]
            out[...] = value.astype(BF16)

        own_pipeline(body, 0, [tok_ref], result_ref)

    def finish_grad():
        gain_sum[...] = jnp.zeros_like(gain_sum)
        shift_sum[...] = jnp.zeros_like(shift_sum)
        dy_sum[...] = jnp.zeros_like(dy_sum)

        def body(step, a, b, c, d, tok, cot, out):
            grad = add_four((a, b, c, d))
            unit_rows, inv_spread = normalize(tok[...].astype(F32))
            dy = cot[...].astype(F32)
            along = grad * unit_rows
            gain_sum[...] = gain_sum[...] + jnp.sum(along, axis=0, keepdims=True)
            shift_sum[...] = shift_sum[...] + jnp.sum(grad, axis=0, keepdims=True)
            dy_sum[...] = dy_sum[...] + jnp.sum(dy, axis=0, keepdims=True)
            scaled = grad * gain_v[...]
            centered = (
                scaled
                - jnp.mean(scaled, axis=-1, keepdims=True)
                - unit_rows * jnp.mean(along * gain_v[...], axis=-1, keepdims=True)
            )
            out[...] = dy + inv_spread * centered

        own_pipeline(body, 1, [tok_ref, cot_ref], grad_ref)

    def small_move(number, src, dst, peer):
        return remote(src, dst, small_send.at[number], small_recv.at[number], peer)

    def sum_small():
        vector[...] = jnp.zeros_like(vector)
        for l in range(lines):
            for q in range(QUARTERS):
                d = l * QUARTERS + q
                place = slice(d * each, (d + 1) * each)
                for number, ref in enumerate((gain_sum, shift_sum, dy_sum)):
                    vector[q, l, number : number + 1, :each] = ref[:, place]
        for i in range(lines):
            owner = quarter * lines + i
            q, l = owner % QUARTERS, owner // QUARTERS
            for k in range(3):
                start = k * wide + i * in_each
                vector[q, l, 3 + k : 4 + k, :in_each] = proj_sum_ref[:, start : start + in_each]
            for r in range(up_each // up_low):
                start = i * up_each + r * up_low
                vector[q, l, 6 + r : 7 + r, :up_low] = pre_sum_ref[:, start : start + up_low]
        first = [
            small_move(j - 1, vector.at[quarter ^ j], vector_land.at[j - 1], (dp ^ j, mp))
            for j in (1, 2, 3)
        ]
        for copy in first:
            copy.start()
        for copy in first:
            copy.wait()
        part[...] = (vector[quarter] + vector_land[0]) + (vector_land[1] + vector_land[2])
        second = [
            small_move(
                2 + k, part.at[lax.rem(line + k, lines)], part_land.at[k - 1], in_line(k)
            )
            for k in range(1, lines)
        ]
        for copy in second:
            copy.start()
        total = part[line]
        for k, copy in enumerate(second):
            copy.wait()
            total = total + part_land[k]
        own_small_ref[...] = total
        third = small_move(2 + lines, own_small_ref, aside_land, aside)
        third.start()
        third.wait()
        row = lax.broadcasted_iota(jnp.int32, total.shape, 0)
        own_small_ref[...] = jnp.where(row < 3, total + aside_land[...], total)

    begin_swap(0, 1)
    send_rows(0, 1, 2)
    own_rows[0].start()
    own_rows[1].start()
    proj_sum_ref[...] = jnp.zeros_like(proj_sum_ref)
    end_swap(0, 1)
    start_line(1, 0, 1)
    send_rows(0, 0)
    begin_swap(2, 3, 4, 5)
    line_step(1, 0, 1)
    begin_swap(6)
    pass_on(0)
    send_rows(1, 0)
    end_swap(2, 3, 4, 5)
    start_line(1, 2)
    line_step(2, 0, 1)
    hand_over(0)
    send_rows(1, 1, 2)
    all_rows(0)
    line_rest(3, 0)
    fetch = pltpu.make_async_copy(smalls_ref, small_v, local_sem.at[9])
    fetch.start()
    fetch.wait()
    small_f[...] = small_v[...].astype(F32)
    for d in range(lines * QUARTERS):
        place = slice(d * each, (d + 1) * each)
        gain_v[:, place] = small_f[d * tall : d * tall + 1, :each]
        shift_v[:, place] = small_f[d * tall + 1 : d * tall + 2, :each]
        bias = small_f[d * tall + 2 : d * tall + 3, :each]
        out_bias_v[:, place] = bias + small_f[d * tall + 3 : d * tall + 4, :each]
    for i in range(lines):
        top = pl.multiple_of((quarter * lines + i) * tall, tall)
        block = small_f[pl.ds(top, tall), :]
        for k in range(3):
            start = k * wide + i * in_each
            in_bias_v[:, start : start + in_each] = block[4 + k : 5 + k, :in_each]
        for r in range(up_each // up_low):
            start = i * up_each + r * up_low
            up_bias_v[:, start : start + up_low] = block[7 + r : 8 + r, :up_low]
    normalize_rows()
    line_rest(3, 1)

    def act_1():
        pass_on(1)
        line_step(1, 2)

    activate({4: act_1})
    line_step(2, 2)
    end_swap(6)
    start_line(1, 3)
    hand_over(1)
    all_rows(1)
    weight_grad("far", dy_ref, act_ref, unit, 0)
    sum_start(0, 1)
    weight_grad("rest", dy_ref, act_ref, unit, 0)
    line_rest(3, 2)

    def att_3():
        line_step(1, 3)
        sum_step(0, 1)

    attend({3: att_3})
    weight_grad("far", dy_ref, mixed_ref, wide, 1, 3 * wide)
    line_step(2, 3)
    weight_grad("far", normed_ref, proj_ref, 3 * wide, 1, 0)
    sum_start(1, 1)
    weight_grad("rest", normed_ref, proj_ref, 3 * wide, 1, 0)
    weight_grad("rest", dy_ref, mixed_ref, wide, 1, 3 * wide)
    sum_step(0, 2)
    line_rest(3, 3)
    forward_rows(1 - core, False)
    to_twin(0)
    gate_back({})
    weight_grad("far", normed_ref, pre_ref, unit, 2)
    sum_start(2, 1)
    sum_total(0, 3)
    arrive("twin", 0)
    forward_rows(core, True)
    to_owners(0)
    sum_step(1, 1)
    backward_rows(1 - core, False)
    to_twin(1)
    weight_grad("rest", normed_ref, pre_ref, unit, 2)
    sum_step(2, 1)
    arrive("twin", 1)
    backward_rows(core, True)
    to_owners(1)
    sum_step(1, 2)
    sum_step(2, 2)
    sum_total(1, 3)
    arrive("owner", 1)
    finish_grad()
    sum_total(2, 3)
    arrive("owner", 0)
    finish_result()
    sum_small()

    for key in list(expected):
        arrive(*key)
    for wait in pending:
        wait()


def run_layer(lines, team, tokens, cotangent, in_weight, out_weight, up_weight, down_weight, small, table):
    rows, width = tokens.shape
    depth = out_weight.shape[0]
    wide = out_weight.shape[1] // QUARTERS
    unit = up_weight.shape[1] // QUARTERS
    chunk = QUARTERS * depth
    whole = lines * chunk
    count = team * rows
    smalls = lines * QUARTERS * small.shape[0]
    steps = max(lines - 1, 1)
    anywhere = pl.BlockSpec(memory_space=pl.ANY)
    inside = pl.BlockSpec(memory_space=pltpu.VMEM)

    def low(*shape):
        return jax.ShapeDtypeStruct(shape, BF16)

    outs = [
        low(count, width),
        low(count, width),
        low(whole, 4 * wide),
        low(whole, unit),
        low(whole, unit),
        low(smalls, 128),
        low(count, width),
        low(count, unit),
        low(count, unit),
        low(count, wide),
        low(count, 3 * wide),
        low(count, unit),
        low(3, width, unit),
        low(3, 2, steps, chunk, unit),
        low(3, 2, steps, chunk, unit),
        low(3, chunk, unit),
        low(2, count // 2, width),
        low(2, count // 2, width),
        low(2, count // 2, width),
        low(2, 3, rows, width),
        low(rows, width),
        jax.ShapeDtypeStruct((rows, width), F32),
        low(depth, QUARTERS * unit),
        low(depth, QUARTERS * unit),
        low(3, depth, QUARTERS * wide),
        low(depth, QUARTERS * wide),
    ]
    tile = (8, 128)
    dma = pltpu.SemaphoreType.DMA
    results = pl.pallas_call(
        functools.partial(layer_kernel, lines),
        out_shape=outs + [jax.ShapeDtypeStruct(tile, F32)],
        in_specs=[anywhere] * 7 + [inside],
        out_specs=[anywhere] * len(outs) + [inside],
        scratch_shapes=[
            pltpu.VMEM((1, 3 * wide), F32),
            pltpu.VMEM((1, unit), F32),
            pltpu.VMEM((1, width), F32),
            pltpu.VMEM((1, width), F32),
            pltpu.VMEM((1, width), F32),
            pltpu.VMEM((QUARTERS, lines) + tile, F32),
            pltpu.VMEM((3, lines) + tile, F32),
            pltpu.VMEM((lines,) + tile, F32),
            pltpu.VMEM((steps,) + tile, F32),
            pltpu.VMEM(tile, F32),
            pltpu.VMEM((smalls, 128), BF16),
            pltpu.VMEM((smalls, 128), F32),
            pltpu.VMEM((1, width), F32),
            pltpu.VMEM((1, width), F32),
            pltpu.VMEM((1, width), F32),
            pltpu.VMEM((1, 3 * wide), F32),
            pltpu.VMEM((1, unit), F32),
            dma((22,)),
            dma((7, 3)),
            dma((7, 3)),
            dma((2, 9)),
            dma((2, 9)),
            dma((4, 2, steps)),
            dma((4, 2, steps)),
            dma((3, 2, steps)),
            dma((3, 2, steps)),
            dma((3, 4, 3)),
            dma((3, 4, 3)),
            dma((2,)),
            dma((2,)),
            dma((2, 3)),
            dma((2, 3)),
            dma((lines + 3,)),
            dma((lines + 3,)),
        ],
        compiler_params=pltpu.CompilerParams(
            collective_id=1, has_side_effects=True, vmem_limit_bytes=VMEM_BYTES
        ),
    )(tokens, cotangent, in_weight, out_weight, up_weight, down_weight, small, table)
    return results[20:]


def smooth_gate(u):
    slope = math.sqrt(2.0 / math.pi)
    square = u * u
    curve = jnp.tanh(slope * (u + 0.044715 * (u * square)))
    rise = 0.5 * (1.0 + curve)
    bend = 0.5 * u * (1.0 - curve * curve) * (slope * (1.0 + 3.0 * 0.044715 * square))
    return u * rise, rise + bend


def per_device(
    tokens,
    norm_gain,
    norm_shift,
    in_weight,
    in_bias,
    out_weight,
    out_bias,
    up_weight,
    up_bias,
    down_weight,
    down_bias,
    cotangent,
):
    n_dp = lax.axis_size("dp")
    n_mp = lax.axis_size("mp")
    lines = n_dp // QUARTERS
    own_rows, width = tokens.shape
    each = norm_gain.shape[0]
    in_each = in_bias.shape[1]
    up_each = up_bias.shape[0]
    wide = out_weight.shape[1] // QUARTERS

    def row(vector):
        return jnp.pad(vector, (0, -vector.shape[0] % 128)).reshape(-1, 128)

    small = jnp.concatenate(
        [row(norm_gain), row(norm_shift), row(out_bias), row(down_bias)]
        + [row(in_bias[k]) for k in range(3)]
        + [row(up_bias)]
    )
    small = jnp.pad(small, ((0, SMALL - small.shape[0]), (0, 0)))
    table = rotary_tables(n_mp * own_rows, wide // HEAD)
    outcome, grad_input, grad_down, grad_up, grad_in, grad_out, owned = run_layer(
        lines, QUARTERS * n_mp, tokens, cotangent, in_weight, out_weight, up_weight, down_weight, small, table
    )
    own_bias = owned[2, :each]
    return (
        outcome,
        grad_input,
        owned[0, :each],
        owned[1, :each],
        grad_in.astype(F32),
        owned[3:6, :in_each],
        grad_out.astype(F32),
        own_bias,
        grad_up.astype(F32),
        owned[6:8, : min(up_each, 128)].reshape(-1)[:up_each],
        grad_down.astype(F32),
        own_bias,
    )


def solution(mesh):
    return jax.shard_map(
        per_device,
        mesh=mesh,
        in_specs=(
            P(("dp", "mp"), None),
            P("dp"),
            P("dp"),
            P(None, "dp", "mp"),
            P(None, ("mp", "dp")),
            P("dp", "mp"),
            P("dp"),
            P("dp", "mp"),
            P(("mp", "dp")),
            P("dp", "mp"),
            P("dp"),
            P(("dp", "mp"), None),
        ),
        out_specs=(
            P(("dp", "mp"), None),
            P(("dp", "mp"), None),
            P("dp"),
            P("dp"),
            P(None, "dp", "mp"),
            P(None, ("mp", "dp")),
            P("dp", "mp"),
            P("dp"),
            P("dp", "mp"),
            P(("mp", "dp")),
            P("dp", "mp"),
            P("dp"),
        ),
        check_vma=False,
    )
```
